256 devices in a mesh: cell: 32 (over y, z), view: 8 (over x, core).
Axes of the slice: x: 4, y: 4, z: 8, core: 2. Of those that a mesh axis runs over, the one named last changes fastest.
Arguments:
- gaussians: float32 [53, 262144], P(None, ('cell', 'view'))
- moment_one: float32 [53, 262144], P(None, ('cell', 'view')), may hold values from -4 to 4
- moment_two: float32 [53, 262144], P(None, ('cell', 'view')), may hold values from 0.01 to 1
- cameras: float32 [2, 2, 4], replicated, as said below
- target: bfloat16 [512, 8, 3, 256], P('cell', 'view'), may hold values from 0 to 1
- gauss_ids: int32 [32, 512, 8, 16], P('cell', None, 'view'), may hold values from 0 to 8191, as said below
- tile_counts: int32 [32, 512, 8], P('cell', None, 'view'), may hold values from 1 to 16
- intersection_slots: int32 [32, 32, 8, 2], P(None, None, 'view'), may hold values from -1 to 15, as said below
- depth_order: int32 [512, 8, 32], P('cell', 'view'), may hold values from 0 to 31, as said below
Outputs:
- rendered: float32 [512, 8, 3, 256], P('cell', 'view')
- new_gaussians: float32 [53, 262144], P(None, ('cell', 'view'))
- new_moment_one: float32 [53, 262144], P(None, ('cell', 'view'))
- new_moment_two: float32 [53, 262144], P(None, ('cell', 'view'))
The draws below stay inside these ranges and needn't reach their ends.
Inputs may be any that keep to these rules, and one draw needn't show every extreme that they name: `gauss_ids`: the live entries of a list are distinct and increasing; over all lists of a cell no Gaussian is named by two live slots; entries at slots at or after the list's count are not read. `intersection_slots`: each list holds a run of consecutive tile offsets within the owner's 16 tiles, followed by -1 for empty slots. `depth_order`: each row is a permutation of the cells. `cameras`: the cross product of the two camera rows' first three entries has a positive third component.
All inputs are finite; a program needn't handle non-finite values.
Results may differ from the reference program's by a relative error of at most 0.0003.
Values sent between devices are 32-bit elements; how exact they have to be, the bound alone decides.
A program may use at most 128 MiB of HBM per device.

```python
import math
import jax
import jax.numpy as jnp
from jax import lax

COEF = 48
PARAMS = 53
G_DEV = 1024
G_CELL = 8192
GAUSS = 262144
OWN = 16
CAP = 2
TILE_ROWS = 512
PER_LIST = 16
TSIDE = 16
PIX = 256
TROW = 32
N_CELL = 32
N_VIEW = 8


def camera_rows(key):
    key = jax.random.fold_in(key, 12)
    noise = jax.random.uniform(key, (2, 2, 4), jnp.float32, minval=-0.1, maxval=0.1)
    width = float(TROW * TSIDE)
    height = float(N_VIEW // 2 * N_CELL * OWN // TROW * TSIDE)
    base = jnp.array([[[1.0, 0.0, 0.2, 0.0], [0.0, 1.0, 0.2, 0.0]]], jnp.float32)
    scales = jnp.array([[[width], [height]]], jnp.float32)
    return (base + noise) * scales


def shuffled_gauss(subkey):
    return jax.random.permutation(subkey, G_CELL).astype(jnp.int32)


def shuffled_cells(subkey):
    return jax.random.permutation(subkey, N_CELL).astype(jnp.int32)


def layout_lists(key):
    key = jax.random.fold_in(key, 21)
    keys = jax.random.split(key, 10)
    cells = jnp.arange(N_CELL, dtype=jnp.int32)
    groups = jnp.arange(N_VIEW, dtype=jnp.int32)
    slot_k = jnp.arange(CAP, dtype=jnp.int32)
    items = jnp.arange(PER_LIST, dtype=jnp.int32)
    offsets = jnp.arange(OWN, dtype=jnp.int32)
    first_group = (groups == 0)[None, None, :]
    own_pair = (cells[:, None] == cells[None, :])[:, :, None] & first_group
    next_pair = ((cells[:, None] + 1) % N_CELL == cells[None, :])[:, :, None] & first_group
    run_len = jax.random.randint(keys[0], (N_CELL, N_CELL, N_VIEW), 0, CAP + 1)
    run_len = jnp.where(own_pair, CAP, jnp.where(next_pair, 0, run_len)).astype(jnp.int32)
    start_raw = jax.random.randint(keys[1], (N_CELL, N_CELL, N_VIEW), 0, 1048576)
    run_start = jnp.where(own_pair, OWN - CAP, start_raw % (OWN - run_len + 1)).astype(jnp.int32)
    live_run = slot_k[None, None, None, :] < run_len[..., None]
    intersection = jnp.where(live_run, run_start[..., None] + slot_k[None, None, None, :], -1).astype(jnp.int32)
    slot_counts = jax.random.randint(keys[2], (N_CELL, N_CELL, N_VIEW, CAP), 1, PER_LIST + 1)
    forced = own_pair[..., None] & (slot_k == 0)[None, None, None, :]
    slot_counts = jnp.where(forced, PER_LIST, slot_counts).astype(jnp.int32)
    live_counts = jnp.where(live_run, slot_counts, 0).astype(jnp.int32)
    flat_counts = live_counts.reshape(N_CELL, -1)
    starts = (jnp.cumsum(flat_counts, axis=1) - flat_counts).reshape(live_counts.shape)
    perms = jax.vmap(shuffled_gauss)(jax.random.split(keys[3], N_CELL))
    positions = starts[..., None] + items[None, None, None, None, :]
    live_item = items[None, None, None, None, :] < live_counts[..., None]
    safe_pos = jnp.minimum(positions, G_CELL - 1).reshape(N_CELL, -1)
    picked = jnp.take_along_axis(perms, safe_pos, axis=1).reshape(positions.shape)
    named = jnp.where(live_item, picked, G_CELL)
    ordered = jnp.sort(named, axis=-1)
    slot_lists = jnp.where(ordered < G_CELL, ordered, G_CELL - 1).astype(jnp.int32)
    choose_k = offsets[None, None, None, :] - run_start[..., None]
    row_listed = (choose_k >= 0) & (choose_k < run_len[..., None])
    safe_k = jnp.clip(choose_k, 0, CAP - 1).astype(jnp.int32)
    full_k = jnp.broadcast_to(safe_k[..., None], (N_CELL, N_CELL, N_VIEW, OWN, PER_LIST))
    row_lists = jnp.take_along_axis(slot_lists, full_k, axis=3)
    row_counts = jnp.take_along_axis(slot_counts, safe_k, axis=3)
    filler_ids = jax.random.randint(keys[4], (N_CELL, N_CELL, N_VIEW, OWN, PER_LIST), 0, G_CELL)
    filler_counts = jax.random.randint(keys[5], (N_CELL, N_CELL, N_VIEW, OWN), 1, PER_LIST + 1)
    id_rows = jnp.where(row_listed[..., None], row_lists, filler_ids)
    count_rows = jnp.where(row_listed, row_counts, filler_counts)
    gauss_ids = jnp.transpose(id_rows, (0, 1, 3, 2, 4)).reshape(N_CELL, N_CELL * OWN, N_VIEW, PER_LIST)
    tile_counts = jnp.transpose(count_rows, (0, 1, 3, 2)).reshape(N_CELL, N_CELL * OWN, N_VIEW)
    dump_ids = jnp.where(live_item, picked, G_CELL).astype(jnp.int32)
    full_shape = positions.shape
    cell_index = jnp.broadcast_to(cells[:, None, None, None, None], full_shape)
    group_value = jnp.broadcast_to(groups[None, None, :, None, None], full_shape)
    row_base = cells[None, :, None, None] * OWN + run_start[..., None] + slot_k[None, None, None, :]
    row_value = jnp.broadcast_to(row_base[..., None], full_shape)
    home_group = jax.random.randint(keys[6], (N_CELL, G_CELL + 1), 0, N_VIEW)
    home_group = home_group.at[cell_index, dump_ids].set(group_value)[:, :G_CELL].astype(jnp.int32)
    home_row = jax.random.randint(keys[7], (N_CELL, G_CELL + 1), 0, N_CELL * OWN)
    home_row = home_row.at[cell_index, dump_ids].set(row_value)[:, :G_CELL].astype(jnp.int32)
    base_rank = jax.vmap(shuffled_cells)(jax.random.split(keys[8], 2))
    view_of_group = groups // (N_VIEW // 2)
    jitter = jax.random.randint(keys[9], (N_CELL * OWN, N_VIEW, N_CELL), 0, 6)
    scores = (base_rank[view_of_group][None, :, :] * 4 + jitter) * N_CELL + cells[None, None, :]
    depth_order = jnp.argsort(scores, axis=-1).astype(jnp.int32)
    depth_rank = jnp.argsort(depth_order, axis=-1).astype(jnp.int32)
    return (intersection, gauss_ids, tile_counts, depth_order, home_group, home_row, depth_rank)


def draw_gaussians(key, part):
    camera = camera_rows(key)
    layout = layout_lists(key)
    home_group, home_row, depth_rank = (layout[4], layout[5], layout[6])
    key = jax.random.fold_in(key, 11)
    subkeys = jax.random.split(key, 5)
    number = N_CELL * N_VIEW * G_DEV
    grid_shape = (N_CELL, N_VIEW * G_DEV)
    half = N_VIEW // 2
    cells = jnp.arange(N_CELL, dtype=jnp.int32)
    which_view = home_group // half
    window = home_group % half * (N_CELL * OWN) + home_row
    anchor_x = (window % TROW * TSIDE).astype(jnp.float32)
    anchor_y = (window // TROW * TSIDE).astype(jnp.float32)
    inner_x = TSIDE * jax.random.uniform(subkeys[0], grid_shape, jnp.float32)
    inner_y = TSIDE * jax.random.uniform(subkeys[1], grid_shape, jnp.float32)
    coeffs = 0.3 * jax.random.normal(subkeys[2], (COEF, number), jnp.float32)
    screen_x = anchor_x + inner_x
    screen_y = anchor_y + inner_y
    cell_rank = depth_rank[home_row, home_group, cells[:, None]].astype(jnp.float32)
    gauss_frac = jnp.arange(N_VIEW * G_DEV, dtype=jnp.float32) / float(N_VIEW * G_DEV)
    depth = (cell_rank + 0.1 + 0.8 * gauss_frac[None, :]) / float(N_CELL)
    rows = camera[which_view]
    rhs_x = screen_x - rows[..., 0, 2] * depth - rows[..., 0, 3]
    rhs_y = screen_y - rows[..., 1, 2] * depth - rows[..., 1, 3]
    determinant = rows[..., 0, 0] * rows[..., 1, 1] - rows[..., 0, 1] * rows[..., 1, 0]
    centre_x = (rows[..., 1, 1] * rhs_x - rows[..., 0, 1] * rhs_y) / determinant
    centre_y = (rows[..., 0, 0] * rhs_y - rows[..., 1, 0] * rhs_x) / determinant
    centres = jnp.stack([centre_x.reshape(-1), centre_y.reshape(-1), depth.reshape(-1)], axis=0)
    log_sigma = jax.random.uniform(subkeys[3], (1, number), jnp.float32, minval=math.log(1.5), maxval=math.log(4.5))
    logits = jax.random.uniform(subkeys[4], (1, number), jnp.float32, minval=-2.0, maxval=1.0)
    return jnp.concatenate([centres, log_sigma, logits, coeffs], axis=0).astype(jnp.float32)


def draw_cameras(key, part):
    return camera_rows(key).astype(jnp.float32)


def draw_intersection_slots(key, part):
    return layout_lists(key)[0]


def draw_gauss_ids(key, part):
    return layout_lists(key)[1]


def draw_tile_counts(key, part):
    return layout_lists(key)[2]


def draw_depth_order(key, part):
    return layout_lists(key)[3]


def levels(rng, dims, pieces, smallest, largest):
    level = 1.0
    for axis_at, parts in pieces:
        steps = jax.random.uniform(jax.random.fold_in(jax.random.fold_in(rng, 6), axis_at), (parts,), jnp.float32, smallest / len(pieces), largest / len(pieces))
        level = level * jnp.repeat(jnp.exp(steps), dims[axis_at] // parts).reshape((-1,) + (1,) * (len(dims) - 1 - axis_at))
    return level


def normal_values(rng, extent, spread, most, pieces=(), kind=jnp.bfloat16):
    values = jax.random.normal(rng, extent, jnp.float32) * spread
    if len(pieces) > 0:
        values = levels(rng, extent, pieces, -0.22, 0.18) * values
    return jnp.clip(values, min=-most, max=most).astype(kind)


def setup_inputs(seed: int = 0) -> dict:
    key_list = jax.random.split(jax.random.key(seed), 10)
    return {
        "gaussians": draw_gaussians(jax.random.fold_in(key_list[9], 71), 0),
        "moment_one": normal_values(key_list[1], (PARAMS, GAUSS), 0.5, 4.0, ((1, 256),), jnp.float32),
        "moment_two": jnp.clip(jnp.exp(math.log(1.0) - 4.6051702 * jax.random.uniform(key_list[2], (PARAMS, GAUSS), jnp.float32) ** levels(key_list[2], (PARAMS, GAUSS), ((1, 256),), -0.2, 0.2)), 0.01, 1.0),
        "cameras": draw_cameras(jax.random.fold_in(key_list[9], 71), 0),
        "target": jnp.clip(1.0 * jax.random.uniform(key_list[4], (TILE_ROWS, N_VIEW, 3, PIX), jnp.float32) ** levels(key_list[4], (TILE_ROWS, N_VIEW, 3, PIX), ((0, 32), (1, 8)), -0.2, 0.2), 0.0, 1.0).astype(jnp.bfloat16),
        "gauss_ids": draw_gauss_ids(jax.random.fold_in(key_list[9], 71), 0),
        "tile_counts": draw_tile_counts(jax.random.fold_in(key_list[9], 71), 0),
        "intersection_slots": draw_intersection_slots(jax.random.fold_in(key_list[9], 71), 0),
        "depth_order": draw_depth_order(jax.random.fold_in(key_list[9], 71), 0),
    }


band_zero = 0.28209479177387814
band_one = 0.4886025119029199
band_two = (1.0925484305920792, -1.0925484305920792, 0.31539156525252005, -1.0925484305920792, 0.5462742152960396)
band_three = (-0.5900435899266435, 2.890611442640554, -0.4570457994644658, 0.3731763325901154, -0.4570457994644658, 1.445305721320277, -0.5900435899266435)
beta_one = 0.9
beta_two = 0.999
learn_rate = 0.01
adam_eps = 1e-08
adam_step = 10.0

def view_basis(camera):
    normal = jnp.cross(camera[0, :3], camera[1, :3])
    unit_dir = normal / jnp.sqrt(jnp.sum(normal * normal))
    comp_x, comp_y, comp_z = (unit_dir[0], unit_dir[1], unit_dir[2])
    sq_x, sq_y, sq_z = (comp_x * comp_x, comp_y * comp_y, comp_z * comp_z)
    sh_list = [comp_x * 0.0 + band_zero, -band_one * comp_y, band_one * comp_z, -band_one * comp_x, band_two[0] * comp_x * comp_y, band_two[1] * comp_y * comp_z, band_two[2] * (2.0 * sq_z - sq_x - sq_y), band_two[3] * comp_x * comp_z, band_two[4] * (sq_x - sq_y), band_three[0] * comp_y * (3.0 * sq_x - sq_y), band_three[1] * comp_x * comp_y * comp_z, band_three[2] * comp_y * (4.0 * sq_z - sq_x - sq_y), band_three[3] * comp_z * (2.0 * sq_z - 3.0 * sq_x - 3.0 * sq_y), band_three[4] * comp_x * (4.0 * sq_z - sq_x - sq_y), band_three[5] * comp_z * (sq_x - sq_y), band_three[6] * comp_x * (sq_x - 3.0 * sq_y)]
    return jnp.stack(sh_list)

def live_mask(counts_rows, listed, length):
    slot_ids = jnp.arange(length, dtype=jnp.int32)
    return ((slot_ids[None, :] < counts_rows[:, None]) & listed[:, None]).astype(jnp.float32)

def render_tiles(cell_params, list_ids, counts_rows, listed, tile_rows, view_group, cameras, half_views, rows_total):
    camera = lax.dynamic_index_in_dim(cameras, view_group // half_views, 0, keepdims=False)
    picked = jnp.take(cell_params, list_ids, axis=1)
    screen_x = camera[0, 0] * picked[0] + camera[0, 1] * picked[1] + camera[0, 2] * picked[2] + camera[0, 3]
    screen_y = camera[1, 0] * picked[0] + camera[1, 1] * picked[1] + camera[1, 2] * picked[2] + camera[1, 3]
    inv_var = jnp.exp(-2.0 * picked[3])
    opacity = jax.nn.sigmoid(picked[4])
    coeffs = picked[5:].reshape(3, 16, list_ids.shape[0], list_ids.shape[1])
    sh_terms = view_basis(camera)
    colour = 0.5 + jnp.einsum('b,cbrk->crk', sh_terms, coeffs, precision=lax.Precision.HIGHEST)
    window_tile = view_group % half_views * rows_total + tile_rows
    anchor_x = (window_tile % TROW * TSIDE).astype(jnp.float32)
    anchor_y = (window_tile // TROW * TSIDE).astype(jnp.float32)
    pixel_ids = jnp.arange(TSIDE * TSIDE, dtype=jnp.int32)
    off_x = (pixel_ids % TSIDE).astype(jnp.float32) + 0.5
    off_y = (pixel_ids // TSIDE).astype(jnp.float32) + 0.5
    delta_x = anchor_x[:, None, None] + off_x[None, None, :] - screen_x[:, :, None]
    delta_y = anchor_y[:, None, None] + off_y[None, None, :] - screen_y[:, :, None]
    distance = delta_x * delta_x + delta_y * delta_y
    live_slots = live_mask(counts_rows, listed, list_ids.shape[1])
    opacity_px = (opacity * live_slots)[:, :, None] * jnp.exp(-0.5 * distance * inv_var[:, :, None])
    log_keep = jnp.log1p(-opacity_px)
    before = jnp.cumsum(log_keep, axis=1) - log_keep
    weight = opacity_px * jnp.exp(before)
    partial_value = jnp.einsum('crk,rkp->rcp', colour, weight, precision=lax.Precision.HIGHEST)
    through = jnp.exp(lax.optimization_barrier(jnp.sum(log_keep, axis=1)))
    return (partial_value, through, live_slots)

def merge_tiles(colour, through, tile_order):
    colour_t = jnp.transpose(colour, (1, 0, 2, 3))
    through_t = jnp.transpose(through, (1, 0, 2))
    colour_s = jnp.take_along_axis(colour_t, tile_order[:, :, None, None], axis=1)
    through_s = jnp.take_along_axis(through_t, tile_order[:, :, None], axis=1)
    ahead = jnp.cumprod(through_s, axis=1)
    prefix = jnp.concatenate([jnp.ones_like(ahead[:, :1]), ahead[:, :-1]], axis=1)
    return lax.optimization_barrier(jnp.sum(prefix[:, :, None, :] * colour_s, axis=1))

def adam_update(params, gradient, first_moment, second, touched):
    new_first = beta_one * first_moment + (1.0 - beta_one) * gradient
    new_second = beta_two * second + (1.0 - beta_two) * gradient * gradient
    fix_one = 1.0 - beta_one ** adam_step
    fix_two = 1.0 - beta_two ** adam_step
    change = learn_rate * (new_first / fix_one) / (jnp.sqrt(new_second / fix_two) + adam_eps)
    touched_mask = touched > 0.5
    return (jnp.where(touched_mask, params - change, params), jnp.where(touched_mask, new_first, first_moment), jnp.where(touched_mask, new_second, second))

def listed_rows(intersection_slots, cell_index, view_group):
    cell_slots = intersection_slots[cell_index, :, view_group, :]
    matches = cell_slots[:, :, None] == jnp.arange(OWN, dtype=jnp.int32)[None, None, :]
    return jnp.any(matches, axis=1).reshape(-1)

def reference(gaussians, moment_one, moment_two, cameras, target, gauss_ids, tile_counts, intersection_slots, depth_order):
    half_views = N_VIEW // 2
    all_rows = jnp.arange(TILE_ROWS, dtype=jnp.int32)
    cell_list = jnp.arange(N_CELL, dtype=jnp.int32)

    def image_of(params):
        images = []
        for view_group in range(N_VIEW):

            def cell_render(cell_index):
                cell_params = lax.dynamic_slice_in_dim(params, cell_index * G_CELL, G_CELL, 1)
                listed = listed_rows(intersection_slots, cell_index, view_group)
                partial_value, through, unused = render_tiles(cell_params, gauss_ids[cell_index, :, view_group, :], tile_counts[cell_index, :, view_group], listed, all_rows, view_group, cameras, half_views, TILE_ROWS)
                return (partial_value, through)
            partial_value, through = lax.map(jax.checkpoint(cell_render), cell_list)
            images.append(merge_tiles(partial_value, through, depth_order[:, view_group, :]))
        return jnp.stack(images, axis=1)
    rendered, pull_back = jax.vjp(image_of, gaussians)
    gradient = pull_back(rendered - target.astype(jnp.float32))[0]

    def touch_cell(cell_index):
        touch_count = jnp.zeros((G_CELL,), jnp.float32)
        for view_group in range(N_VIEW):
            listed = listed_rows(intersection_slots, cell_index, view_group)
            live_slots = live_mask(tile_counts[cell_index, :, view_group], listed, PER_LIST)
            touch_count = touch_count.at[gauss_ids[cell_index, :, view_group, :].reshape(-1)].add(live_slots.reshape(-1))
        return touch_count
    touched = lax.map(touch_cell, cell_list).reshape(-1)
    new_gaussians, new_one, new_two = adam_update(gaussians, gradient, moment_one, moment_two, touched)
    return (rendered, new_gaussians, new_one, new_two)
```

```python
import jax
import jax.numpy as jnp
from jax import lax
from jax.experimental import pallas as pl
from jax.experimental.pallas import tpu as pltpu
from jax.sharding import PartitionSpec as P

CELLS = 32
VIEWS = 8
HALF_VIEWS = VIEWS // 2
HOME = 1024
OWN = 16
ROWS = 512
PIX = 256
TSIDE = 16
LISTS = 2 * CELLS
SUB = 8
LANES = 128
HIGHS = VIEWS * SUB
F32 = jnp.float32
BF16 = jnp.bfloat16
LARGE = 1e38

band_zero = 0.28209479177387814
band_one = 0.4886025119029199
band_two = (
    1.0925484305920792,
    -1.0925484305920792,
    0.31539156525252005,
    -1.0925484305920792,
    0.5462742152960396,
)
band_three = (
    -0.5900435899266435,
    2.890611442640554,
    -0.4570457994644658,
    0.3731763325901154,
    -0.4570457994644658,
    1.445305721320277,
    -0.5900435899266435,
)
beta_one = 0.9
beta_two = 0.999
learn_rate = 0.01
adam_eps = 1e-08
adam_step = 10.0


def iota(shape, axis):
    return lax.broadcasted_iota(jnp.int32, shape, axis)


def camera_values(cam_ref, which):
    return [[cam_ref[which, row : row + 1, k : k + 1] for k in range(4)] for row in range(2)]


def basis_column(camera):
    a, b = camera
    nx = a[1] * b[2] - a[2] * b[1]
    ny = a[2] * b[0] - a[0] * b[2]
    nz = a[0] * b[1] - a[1] * b[0]
    norm = jnp.sqrt(nx * nx + ny * ny + nz * nz)
    x, y, z = nx / norm, ny / norm, nz / norm
    xx, yy, zz = x * x, y * y, z * z
    terms = [
        x * 0.0 + band_zero,
        -band_one * y,
        band_one * z,
        -band_one * x,
        band_two[0] * x * y,
        band_two[1] * y * z,
        band_two[2] * (2.0 * zz - xx - yy),
        band_two[3] * x * z,
        band_two[4] * (xx - yy),
        band_three[0] * y * (3.0 * xx - yy),
        band_three[1] * x * y * z,
        band_three[2] * y * (4.0 * zz - xx - yy),
        band_three[3] * z * (2.0 * zz - 3.0 * xx - 3.0 * yy),
        band_three[4] * x * (4.0 * zz - xx - yy),
        band_three[5] * z * (xx - yy),
        band_three[6] * x * (xx - 3.0 * yy),
    ]
    row = iota((16, 1), 0)
    column = jnp.zeros((16, 1), F32)
    for at, term in enumerate(terms):
        column = jnp.where(row == at, term, column)
    return column


def split3(x):
    high = x.astype(BF16)
    rest = x - high.astype(F32)
    mid = rest.astype(BF16)
    low = (rest - mid.astype(F32)).astype(BF16)
    return high, mid, low


def dot(a, b, dims=((1,), (0,))):
    return lax.dot_general(a, b, (dims, ((), ())), preferred_element_type=F32)


def rows_to_lists(x):
    t = x.T
    return jnp.concatenate([t[:LISTS], t[LISTS:]], axis=1)


def lists_to_rows(x):
    t = x.T
    return jnp.concatenate([t[:64], t[64:]], axis=1)


def step_kernel(
    g_ref,
    cam_ref,
    tgt_ref,
    ids_ref,
    cnt_ref,
    isl_ref,
    ord_ref,
    rend_ref,
    gout_ref,
    tab_send,
    tab_recv,
    fwd_send,
    fwd_recv,
    bwd_send,
    bwd_recv,
    grad_send,
    grad_recv,
    oh_ref,
    hi_ref,
    v_ref,
    ex_ref,
    ey_ref,
    dy_ref,
    w_ref,
    rho_ref,
    part_ref,
    pre_ref,
    behind_ref,
    gl_ref,
    acc_ref,
    lhs_ref,
    sem_ts,
    sem_tr,
    sem_fs,
    sem_fr,
    sem_bs,
    sem_br,
    sem_gs,
    sem_gr,
):
    me_c = lax.axis_index("cell")
    me_v = lax.axis_index("view")

    def peer_c(d):
        return lax.rem(me_c + d, CELLS)

    def peer_v(d):
        return lax.rem(me_v + d, VIEWS)

    barrier = pltpu.get_barrier_semaphore()

    def greet_cell(d, carry):
        pl.semaphore_signal(
            barrier, inc=1, device_id=(peer_c(d), me_v), device_id_type=pl.DeviceIdType.MESH
        )
        return carry

    def greet_view(d, carry):
        pl.semaphore_signal(
            barrier, inc=1, device_id=(me_c, peer_v(d)), device_id_type=pl.DeviceIdType.MESH
        )
        return carry

    lax.fori_loop(1, VIEWS, greet_view, 0)
    lax.fori_loop(1, CELLS, greet_cell, 0)

    centre = [g_ref[k : k + 1, :] for k in range(3)]
    inv_var = jnp.exp(-2.0 * g_ref[3:4, :])
    opacity = 1.0 / (1.0 + jnp.exp(-g_ref[4:5, :]))
    for which in range(2):
        camera = camera_values(cam_ref, which)
        column = basis_column(camera)
        screen = [
            row[0] * centre[0] + row[1] * centre[1] + row[2] * centre[2] + row[3] for row in camera
        ]
        colour = [
            0.5 + jnp.sum(g_ref[5 + 16 * ch : 21 + 16 * ch, :] * column, axis=0, keepdims=True)
            for ch in range(3)
        ]
        table = jnp.concatenate(
            screen + [inv_var, opacity] + colour + [jnp.zeros((1, HOME), F32)], axis=0
        )
        table = jnp.clip(table, -LARGE, LARGE)
        tab_send[which] = jnp.where(table == table, table, 0.0)

    pl.semaphore_wait(barrier, VIEWS - 1 + CELLS - 1)

    def table_copy(d):
        to = peer_v(d)
        return pltpu.make_async_remote_copy(
            src_ref=tab_send.at[to // HALF_VIEWS],
            dst_ref=tab_recv.at[me_v],
            send_sem=sem_ts.at[d],
            recv_sem=sem_tr.at[me_v],
            device_id=(me_c, to),
            device_id_type=pl.DeviceIdType.MESH,
        )

    def table_start(d, carry):
        table_copy(d).start()
        return carry

    lax.fori_loop(1, VIEWS, table_start, 0)
    tab_recv[me_v] = tab_send[me_v // HALF_VIEWS]

    lane = iota((1, LANES), 1)
    mine = isl_ref[me_c]
    offsets = jnp.concatenate([mine[0:1], mine[1:2], mine[0:1], mine[1:2]], axis=1)
    wanted = jnp.where(offsets >= 0, lax.rem(lane, CELLS) * OWN + offsets, -1)
    pick = (iota((ROWS, LANES), 0) == wanted).astype(F32).astype(BF16)
    all_ids = ids_ref[...]
    packed = jnp.concatenate(
        [
            (all_ids // LANES).astype(F32),
            lax.rem(all_ids, LANES).astype(F32),
            jnp.broadcast_to(cnt_ref[...].astype(F32), (16, ROWS)),
        ],
        axis=0,
    ).astype(BF16)
    picked = dot(packed, pick)
    left = iota((SUB, LANES), 1) < LISTS
    high = jnp.where(left, picked[0:8], picked[8:16])
    low = jnp.where(left, picked[16:24], picked[24:32])
    slot = iota((SUB, LANES), 0) + jnp.where(left, 0, SUB)
    live = slot.astype(F32) < picked[32:40]
    high = jnp.where(live, high, -1.0)
    hi_ref[...] = high
    for kk in range(SUB):
        hot = (iota((LANES, LANES), 0).astype(F32) == low[kk : kk + 1]).astype(F32).astype(BF16)
        for part in range(3):
            oh_ref[part * LANES : (part + 1) * LANES, kk * LANES : (kk + 1) * LANES] = hot

    def table_wait(d, carry):
        pltpu.make_async_remote_copy(
            src_ref=tab_send.at[0],
            dst_ref=tab_recv.at[peer_v(d)],
            send_sem=sem_ts.at[d],
            recv_sem=sem_tr.at[peer_v(d)],
            device_id=(me_c, peer_v(d)),
            device_id_type=pl.DeviceIdType.MESH,
        ).wait_recv()
        return carry

    lax.fori_loop(1, VIEWS, table_wait, 0)

    blocks = []
    for home in range(VIEWS):
        for at in range(SUB):
            value = tab_recv[home, :, at * LANES : (at + 1) * LANES]
            blocks.append(value)
    parts = split3(jnp.concatenate(blocks, axis=0))
    lhs = jnp.concatenate(parts, axis=1)
    chosen = []
    for pair in range(4):
        got = dot(lhs, oh_ref[:, pair * 256 : (pair + 1) * 256])
        for side in range(2):
            hi = hi_ref[2 * pair + side : 2 * pair + side + 1, :]
            total = jnp.zeros((SUB, LANES), F32)
            for at in range(HIGHS):
                total = total + jnp.where(
                    hi == float(at), got[at * SUB : (at + 1) * SUB, side * LANES : (side + 1) * LANES], 0.0
                )
            chosen.append(total)
    lists = rows_to_lists(jnp.concatenate(chosen, axis=0))
    fwd_send[:, 0, :] = lists[:CELLS]
    fwd_send[:, 1, :] = lists[CELLS:]

    def cell_copy(source, target, send, recv, d):
        return pltpu.make_async_remote_copy(
            src_ref=source.at[peer_c(d)],
            dst_ref=target.at[me_c],
            send_sem=send.at[d],
            recv_sem=recv.at[me_c],
            device_id=(peer_c(d), me_v),
            device_id_type=pl.DeviceIdType.MESH,
        )

    def cell_arrived(source, target, send, recv, d):
        return pltpu.make_async_remote_copy(
            src_ref=source.at[peer_c(d)],
            dst_ref=target.at[peer_c(d)],
            send_sem=send.at[d],
            recv_sem=recv.at[peer_c(d)],
            device_id=(peer_c(d), me_v),
            device_id_type=pl.DeviceIdType.MESH,
        )

    def fwd_start(d, carry):
        cell_copy(fwd_send, fwd_recv, sem_fs, sem_fr, d).start()
        return carry

    lax.fori_loop(1, CELLS, fwd_start, 0)
    fwd_recv[me_c] = fwd_send[me_c]

    both = jnp.concatenate([isl_ref[:, 0, :], isl_ref[:, 1, :]], axis=0).astype(F32)
    at_me = jnp.where(iota((LISTS, CELLS), 1) == me_c, both, 0.0)
    tile_half = jnp.sum(at_me, axis=1, keepdims=True)
    tile_col = jnp.concatenate([tile_half, tile_half], axis=0)
    eye = iota((LANES, LANES), 0) == iota((LANES, LANES), 1)
    tile_row = jnp.sum(jnp.where(eye, tile_col, 0.0), axis=0, keepdims=True)
    in_tile = (iota((OWN, LANES), 0).astype(F32) == tile_row).astype(F32)
    order = ord_ref[...].reshape(OWN, CELLS)
    cell_lane = lax.rem(iota((OWN, LANES), 1), CELLS)
    rank = jnp.zeros((OWN, LANES), F32)
    for at in range(CELLS):
        rank = jnp.where(order[:, at : at + 1] == cell_lane, float(at), rank)
    rank_row = jnp.sum(in_tile * rank, axis=0, keepdims=True)
    key_row = 2.0 * rank_row + jnp.where(lane < LISTS, 0.0, 1.0)
    key_col = jnp.sum(jnp.where(eye, key_row, 0.0), axis=1, keepdims=True)
    same = (tile_col == tile_row) & (tile_row >= 0.0)
    ahead = (same & (key_col < key_row)).astype(F32).astype(BF16)
    after = (same & (key_col > key_row)).astype(F32).astype(BF16)
    ahead3 = jnp.concatenate([ahead] * 3, axis=0)
    after3 = jnp.concatenate([after] * 3, axis=0)
    in_tile_b = in_tile.astype(BF16)
    in_tile3 = jnp.concatenate([in_tile_b] * 3, axis=1)
    in_tile3v = jnp.concatenate([in_tile_b] * 3, axis=0)
    tile_int = tile_row.astype(jnp.int32)
    window = lax.rem(me_v, HALF_VIEWS) * ROWS + me_c * OWN + tile_int
    side_at = iota((TSIDE, LANES), 0).astype(F32) + 0.5
    place_x = (lax.rem(window, 32) * TSIDE).astype(F32) + side_at
    place_y = ((window // 32) * TSIDE).astype(F32) + side_at
    acc_ref[...] = jnp.zeros_like(acc_ref)

    def fwd_wait(d, carry):
        cell_arrived(fwd_send, fwd_recv, sem_fs, sem_fr, d).wait_recv()
        return carry

    lax.fori_loop(1, CELLS, fwd_wait, 0)
    v_ref[...] = lists_to_rows(
        jnp.concatenate([fwd_recv[:, 0, :], fwd_recv[:, 1, :]], axis=0)
    )

    def value(kk, j):
        return v_ref[kk * SUB + j : kk * SUB + j + 1, :]

    for kk in range(SUB):
        inv = -0.5 * value(kk, 2)
        dx = place_x - value(kk, 0)
        dy = place_y - value(kk, 1)
        ex_ref[kk] = value(kk, 3) * jnp.exp(inv * (dx * dx))
        ey_ref[kk] = jnp.exp(inv * (dy * dy))
        dy_ref[kk] = dy

    def forward(i, carry):
        rows = pl.ds(pl.multiple_of(i * 32, 32), 32)
        through = jnp.ones((32, LANES), F32)
        second = jnp.ones((32, LANES), F32)
        first = through
        sums = [jnp.zeros((32, LANES), F32) for ch in range(3)]
        for kk in range(SUB):
            ex = ex_ref[kk]
            alpha = jnp.concatenate(
                [ex * ey_ref[kk, pl.ds(2 * i + at, 1), :] for at in range(2)], axis=0
            )
            keep = 1.0 - alpha
            weight = alpha * through
            w_ref[kk, rows, :] = weight
            rho_ref[kk, rows, :] = alpha / keep
            for ch in range(3):
                sums[ch] = sums[ch] + weight * value(kk, 4 + ch)
            through = through * keep
            if kk < 4:
                first = through
            else:
                second = second * keep
        for ch in range(3):
            part_ref[ch, rows, :] = sums[ch]
        pre_ref[rows, :] = jnp.log(first) + jnp.log(second)
        return carry

    lax.fori_loop(0, 8, forward, 0)

    prefix = jnp.exp(dot(jnp.concatenate(split3(pre_ref[...]), axis=1), ahead3))
    pre_ref[...] = prefix
    owed = jnp.zeros((PIX, LANES), F32)
    for ch in range(3):
        seen = prefix * part_ref[ch]
        image = dot(in_tile3, jnp.concatenate(split3(seen), axis=1), ((1,), (1,)))
        rend_ref[pl.ds(2 * ch, OWN, stride=6), :] = image[:, :LANES]
        rend_ref[pl.ds(2 * ch + 1, OWN, stride=6), :] = image[:, LANES:]
        miss = image - tgt_ref[ch].astype(F32)
        miss3 = jnp.concatenate(split3(miss), axis=0)
        pulled = dot(miss3, in_tile3v, ((0,), (0,)))
        gl_ref[ch] = pulled
        owed = owed + seen * pulled
    behind_ref[...] = dot(jnp.concatenate(split3(owed), axis=1), after3)

    def backward(i, carry):
        rows = pl.ds(pl.multiple_of(i * 32, 32), 32)
        prefix = pre_ref[rows, :]
        behind = behind_ref[rows, :]
        pulled = [gl_ref[ch, rows, :] for ch in range(3)]
        for kk in reversed(range(SUB)):
            weight = prefix * w_ref[kk, rows, :]
            gain = (
                pulled[0] * value(kk, 4) + pulled[1] * value(kk, 5) + pulled[2] * value(kk, 6)
            )
            owed = weight * gain
            pull = owed - behind * rho_ref[kk, rows, :]
            behind = behind + owed
            up, down = pull[:16], pull[16:]
            dy_up = dy_ref[kk, pl.ds(2 * i, 1), :]
            dy_down = dy_ref[kk, pl.ds(2 * i + 1, 1), :]
            acc_ref[kk, 0] += up + down
            along = up * dy_up
            along_down = down * dy_down
            acc_ref[kk, 1] += along + along_down
            acc_ref[kk, 2] += along * dy_up + along_down * dy_down
            for ch in range(3):
                tint = weight * pulled[ch]
                acc_ref[kk, 3 + ch] += tint[:16] + tint[16:]
        return carry

    lax.fori_loop(0, 8, backward, 0)

    results = []
    for kk in range(SUB):
        dx = place_x - value(kk, 0)
        inv = value(kk, 2)
        base = acc_ref[kk, 0]
        base_x = base * dx

        def total(x):
            return jnp.sum(x, axis=0, keepdims=True)

        results += [
            inv * total(base_x),
            inv * total(acc_ref[kk, 1]),
            inv * total(base_x * dx + acc_ref[kk, 2]),
            (1.0 - value(kk, 3)) * total(base),
            total(acc_ref[kk, 3]),
            total(acc_ref[kk, 4]),
            total(acc_ref[kk, 5]),
            jnp.zeros((1, LANES), F32),
        ]
    lists = rows_to_lists(jnp.concatenate(results, axis=0))
    bwd_send[:, 0, :] = lists[:CELLS]
    bwd_send[:, 1, :] = lists[CELLS:]

    def bwd_start(d, carry):
        cell_copy(bwd_send, bwd_recv, sem_bs, sem_br, d).start()
        return carry

    lax.fori_loop(1, CELLS, bwd_start, 0)
    bwd_recv[me_c] = bwd_send[me_c]

    def bwd_wait(d, carry):
        cell_arrived(bwd_send, bwd_recv, sem_bs, sem_br, d).wait_recv()
        return carry

    lax.fori_loop(1, CELLS, bwd_wait, 0)

    grads = lists_to_rows(jnp.concatenate([bwd_recv[:, 0, :], bwd_recv[:, 1, :]], axis=0))
    last = iota((SUB, LANES), 0) == SUB - 1
    for kk in range(SUB):
        hi = hi_ref[kk : kk + 1, :]
        piece = split3(jnp.where(last, 1.0, grads[kk * SUB : (kk + 1) * SUB]))
        piece = [x.astype(F32) for x in piece]
        for at in range(0, HIGHS, 2):
            here, there = hi == float(at), hi == float(at + 1)
            for part in range(3):
                lhs_ref[part, at * SUB : (at + 2) * SUB, kk * LANES : (kk + 1) * LANES] = (
                    jnp.concatenate(
                        [jnp.where(here, piece[part], 0.0), jnp.where(there, piece[part], 0.0)],
                        axis=0,
                    ).astype(BF16)
                )
    hot = oh_ref[0:LANES, :]
    spread = dot(lhs_ref[0], hot, ((1,), (1,)))
    spread = spread + dot(lhs_ref[1], hot, ((1,), (1,)))
    spread = spread + dot(lhs_ref[2], hot, ((1,), (1,)))
    for home in range(VIEWS):
        for at in range(SUB):
            row = (home * SUB + at) * SUB
            grad_send[home, :, at * LANES : (at + 1) * LANES] = spread[row : row + SUB]

    def grad_start(d, carry):
        to = peer_v(d)
        pltpu.make_async_remote_copy(
            src_ref=grad_send.at[to],
            dst_ref=grad_recv.at[me_v],
            send_sem=sem_gs.at[d],
            recv_sem=sem_gr.at[me_v],
            device_id=(me_c, to),
            device_id_type=pl.DeviceIdType.MESH,
        ).start()
        return carry

    lax.fori_loop(1, VIEWS, grad_start, 0)
    grad_recv[me_v] = grad_send[me_v]

    def grad_arrived(d):
        return pltpu.make_async_remote_copy(
            src_ref=grad_send.at[peer_v(d)],
            dst_ref=grad_recv.at[peer_v(d)],
            send_sem=sem_gs.at[d],
            recv_sem=sem_gr.at[peer_v(d)],
            device_id=(me_c, peer_v(d)),
            device_id_type=pl.DeviceIdType.MESH,
        )

    def grad_wait(d, carry):
        grad_arrived(d).wait_recv()
        return carry

    lax.fori_loop(1, VIEWS, grad_wait, 0)
    gout_ref[0] = (grad_recv[0] + grad_recv[1]) + (grad_recv[2] + grad_recv[3])
    gout_ref[1] = (grad_recv[4] + grad_recv[5]) + (grad_recv[6] + grad_recv[7])

    def sent_view(d, carry):
        table_copy(d).wait_send()
        grad_arrived(d).wait_send()
        return carry

    def sent_cell(d, carry):
        cell_copy(fwd_send, fwd_recv, sem_fs, sem_fr, d).wait_send()
        cell_copy(bwd_send, bwd_recv, sem_bs, sem_br, d).wait_send()
        return carry

    lax.fori_loop(1, VIEWS, sent_view, 0)
    lax.fori_loop(1, CELLS, sent_cell, 0)


def adam_kernel(grad_ref, cam_ref, g_ref, one_ref, two_ref, new_g, new_one, new_two):
    touched = grad_ref[0, 7:8, :] + grad_ref[1, 7:8, :] > 0.5
    cameras = [camera_values(cam_ref, which) for which in range(2)]
    columns = [basis_column(camera) for camera in cameras]
    fix_one = 1.0 / (1.0 - beta_one**adam_step)
    fix_two = 1.0 / (1.0 - beta_two**adam_step)

    def update(rows, grad):
        first = beta_one * one_ref[rows, :] + (1.0 - beta_one) * grad
        second = beta_two * two_ref[rows, :] + (1.0 - beta_two) * grad * grad
        change = learn_rate * (first * fix_one) / (jnp.sqrt(second * fix_two) + adam_eps)
        new_g[rows, :] = jnp.where(touched, g_ref[rows, :] - change, g_ref[rows, :])
        new_one[rows, :] = jnp.where(touched, first, one_ref[rows, :])
        new_two[rows, :] = jnp.where(touched, second, two_ref[rows, :])

    small = []
    for k in range(3):
        small.append(
            sum(
                cameras[which][row][k] * grad_ref[which, row : row + 1, :]
                for which in range(2)
                for row in range(2)
            )
        )
    for j in (2, 3):
        small.append(grad_ref[0, j : j + 1, :] + grad_ref[1, j : j + 1, :])
    update(slice(0, 5), jnp.concatenate(small, axis=0))
    for ch in range(3):
        j = 4 + ch
        update(
            slice(5 + 16 * ch, 21 + 16 * ch),
            columns[0] * grad_ref[0, j : j + 1, :] + columns[1] * grad_ref[1, j : j + 1, :],
        )


def per_device(
    gaussians,
    moment_one,
    moment_two,
    cameras,
    target,
    gauss_ids,
    tile_counts,
    intersection_slots,
    depth_order,
):
    vmem = pl.BlockSpec(memory_space=pltpu.VMEM)
    sems = pltpu.SemaphoreType.DMA
    rendered, grads = pl.pallas_call(
        step_kernel,
        out_shape=(
            jax.ShapeDtypeStruct((96, LANES), F32),
            jax.ShapeDtypeStruct((2, SUB, HOME), F32),
        ),
        in_specs=[vmem] * 7,
        out_specs=(vmem, vmem),
        scratch_shapes=[
            pltpu.VMEM((2, SUB, HOME), F32),
            pltpu.VMEM((VIEWS, SUB, HOME), F32),
            pltpu.VMEM((CELLS, 2, LANES), F32),
            pltpu.VMEM((CELLS, 2, LANES), F32),
            pltpu.VMEM((CELLS, 2, LANES), F32),
            pltpu.VMEM((CELLS, 2, LANES), F32),
            pltpu.VMEM((VIEWS, SUB, HOME), F32),
            pltpu.VMEM((VIEWS, SUB, HOME), F32),
            pltpu.VMEM((3 * LANES, SUB * LANES), BF16),
            pltpu.VMEM((SUB, LANES), F32),
            pltpu.VMEM((64, LANES), F32),
            pltpu.VMEM((SUB, TSIDE, LANES), F32),
            pltpu.VMEM((SUB, TSIDE, LANES), F32),
            pltpu.VMEM((SUB, TSIDE, LANES), F32),
            pltpu.VMEM((SUB, PIX, LANES), F32),
            pltpu.VMEM((SUB, PIX, LANES), F32),
            pltpu.VMEM((3, PIX, LANES), F32),
            pltpu.VMEM((PIX, LANES), F32),
            pltpu.VMEM((PIX, LANES), F32),
            pltpu.VMEM((3, PIX, LANES), F32),
            pltpu.VMEM((SUB, 6, TSIDE, LANES), F32),
            pltpu.VMEM((3, HIGHS * SUB, SUB * LANES), BF16),
            sems((VIEWS,)),
            sems((VIEWS,)),
            sems((CELLS,)),
            sems((CELLS,)),
            sems((CELLS,)),
            sems((CELLS,)),
            sems((VIEWS,)),
            sems((VIEWS,)),
        ],
        compiler_params=pltpu.CompilerParams(
            collective_id=0, has_side_effects=True, vmem_limit_bytes=40 * 1024 * 1024
        ),
        name="splat_step",
    )(
        gaussians,
        cameras,
        jnp.transpose(target[:, 0], (1, 0, 2)),
        jnp.transpose(gauss_ids[0, :, 0, :], (1, 0)),
        tile_counts.reshape(1, ROWS),
        jnp.transpose(intersection_slots[:, :, 0, :], (0, 2, 1)),
        depth_order,
    )
    shape = jax.ShapeDtypeStruct(gaussians.shape, F32)
    new_gaussians, new_one, new_two = pl.pallas_call(
        adam_kernel,
        out_shape=(shape, shape, shape),
        in_specs=[vmem] * 5,
        out_specs=(vmem,) * 3,
        compiler_params=pltpu.CompilerParams(vmem_limit_bytes=20 * 1024 * 1024),
        name="adam",
    )(grads, cameras, gaussians, moment_one, moment_two)
    return (rendered.reshape(OWN, 1, 3, PIX), new_gaussians, new_one, new_two)


def solution(mesh):
    placed = (
        P(None, ("cell", "view")),
        P(None, ("cell", "view")),
        P(None, ("cell", "view")),
        P(),
        P("cell", "view", None, None),
        P("cell", None, "view", None),
        P("cell", None, "view"),
        P(None, None, "view", None),
        P("cell", "view", None),
    )
    return jax.shard_map(
        per_device,
        mesh=mesh,
        in_specs=placed,
        out_specs=(
            P("cell", "view", None, None),
            P(None, ("cell", "view")),
            P(None, ("cell", "view")),
            P(None, ("cell", "view")),
        ),
        check_vma=False,
    )
```

```python
import jax
import jax.numpy as jnp
from jax import lax
from jax.experimental import pallas as pl
from jax.experimental.pallas import tpu as pltpu
from jax.sharding import PartitionSpec as P

CELLS = 32
VIEWS = 8
HALF_VIEWS = VIEWS // 2
HOME = 1024
OWN = 16
ROWS = 512
PIX = 256
TSIDE = 16
LISTS = 2 * CELLS
SUB = 8
LANES = 128
HIGHS = VIEWS * SUB
F32 = jnp.float32
BF16 = jnp.bfloat16
LARGE = 1e38

band_zero = 0.28209479177387814
band_one = 0.4886025119029199
band_two = (
    1.0925484305920792,
    -1.0925484305920792,
    0.31539156525252005,
    -1.0925484305920792,
    0.5462742152960396,
)
band_three = (
    -0.5900435899266435,
    2.890611442640554,
    -0.4570457994644658,
    0.3731763325901154,
    -0.4570457994644658,
    1.445305721320277,
    -0.5900435899266435,
)
beta_one = 0.9
beta_two = 0.999
learn_rate = 0.01
adam_eps = 1e-08
adam_step = 10.0


def iota(shape, axis):
    return lax.broadcasted_iota(jnp.int32, shape, axis)


def camera_values(cam_ref, which):
    return [[cam_ref[which, row : row + 1, k : k + 1] for k in range(4)] for row in range(2)]


def basis_column(camera):
    a, b = camera
    nx = a[1] * b[2] - a[2] * b[1]
    ny = a[2] * b[0] - a[0] * b[2]
    nz = a[0] * b[1] - a[1] * b[0]
    norm = jnp.sqrt(nx * nx + ny * ny + nz * nz)
    x, y, z = nx / norm, ny / norm, nz / norm
    xx, yy, zz = x * x, y * y, z * z
    terms = [
        x * 0.0 + band_zero,
        -band_one * y,
        band_one * z,
        -band_one * x,
        band_two[0] * x * y,
        band_two[1] * y * z,
        band_two[2] * (2.0 * zz - xx - yy),
        band_two[3] * x * z,
        band_two[4] * (xx - yy),
        band_three[0] * y * (3.0 * xx - yy),
        band_three[1] * x * y * z,
        band_three[2] * y * (4.0 * zz - xx - yy),
        band_three[3] * z * (2.0 * zz - 3.0 * xx - 3.0 * yy),
        band_three[4] * x * (4.0 * zz - xx - yy),
        band_three[5] * z * (xx - yy),
        band_three[6] * x * (xx - 3.0 * yy),
    ]
    row = iota((16, 1), 0)
    column = jnp.zeros((16, 1), F32)
    for at, term in enumerate(terms):
        column = jnp.where(row == at, term, column)
    return column


def split3(x):
    high = x.astype(BF16)
    rest = x - high.astype(F32)
    mid = rest.astype(BF16)
    low = (rest - mid.astype(F32)).astype(BF16)
    return high, mid, low


def split2(x):
    high = x.astype(BF16)
    return high, (x - high.astype(F32)).astype(BF16)


def dot(a, b, dims=((1,), (0,))):
    return lax.dot_general(a, b, (dims, ((), ())), preferred_element_type=F32)


def rows_to_lists(x):
    t = x.T
    return jnp.concatenate([t[:LISTS], t[LISTS:]], axis=1)


def lists_to_rows(x):
    t = x.T
    return jnp.concatenate([t[:64], t[64:]], axis=1)


def step_kernel(
    g_hbm,
    one_hbm,
    two_hbm,
    cam_hbm,
    tgt_hbm,
    ids_hbm,
    cnt_hbm,
    isl_hbm,
    ord_hbm,
    rend_ref,
    gout_ref,
    basis_ref,
    cam_ref,
    g_ref,
    one_ref,
    two_ref,
    tgt_ref,
    ids_ref,
    cnt_ref,
    isl_ref,
    ord_ref,
    tab_send,
    tab_recv,
    fwd_send,
    fwd_recv,
    bwd_send,
    bwd_recv,
    grad_send,
    grad_recv,
    oh_ref,
    hi_ref,
    v_ref,
    ex_ref,
    ey_ref,
    dy_ref,
    w_ref,
    rho_ref,
    part_ref,
    pre_ref,
    behind_ref,
    gl_ref,
    acc_ref,
    lhs_ref,
    sem_ts,
    sem_tr,
    sem_f,
    sem_b,
    sem_gs,
    sem_gr,
    sem_in,
):
    loads = [
        pltpu.make_async_copy(source, target, sem_in.at[at])
        for at, (source, target) in enumerate(
            (
                (g_hbm, g_ref),
                (cam_hbm, cam_ref),
                (isl_hbm, isl_ref),
                (ids_hbm, ids_ref),
                (cnt_hbm, cnt_ref),
                (ord_hbm, ord_ref),
                (tgt_hbm, tgt_ref),
                (one_hbm, one_ref),
                (two_hbm, two_ref),
            )
        )
    ]
    for load in loads[:7]:
        load.start()
    me_c = lax.axis_index("cell")
    me_v = lax.axis_index("view")

    def peer_c(d):
        return lax.rem(me_c + lax.rem(d + 10, CELLS - 1) + 1, CELLS)

    def peer_v(d):
        return lax.rem(me_v + d, VIEWS)

    barrier = pltpu.get_barrier_semaphore()

    def greet_cell(d, carry):
        pl.semaphore_signal(
            barrier, inc=1, device_id=(peer_c(d), me_v), device_id_type=pl.DeviceIdType.MESH
        )
        return carry

    def greet_view(d, carry):
        pl.semaphore_signal(
            barrier, inc=1, device_id=(me_c, peer_v(d)), device_id_type=pl.DeviceIdType.MESH
        )
        return carry

    lax.fori_loop(1, CELLS, greet_cell, 0)
    lax.fori_loop(1, VIEWS, greet_view, 0)
    for load in loads[:7]:
        load.wait()
    for load in loads[7:]:
        load.start()

    centre = [g_ref[k : k + 1, :] for k in range(3)]
    inv_var = jnp.exp(-2.0 * g_ref[3:4, :])
    opacity = 1.0 / (1.0 + jnp.exp(-g_ref[4:5, :]))
    for which in range(2):
        camera = camera_values(cam_ref, which)
        column = basis_column(camera)
        basis_ref[which] = jnp.broadcast_to(column, (16, LANES))
        screen = [
            row[0] * centre[0] + row[1] * centre[1] + row[2] * centre[2] + row[3] for row in camera
        ]
        colour = [
            0.5 + jnp.sum(g_ref[5 + 16 * ch : 21 + 16 * ch, :] * column, axis=0, keepdims=True)
            for ch in range(3)
        ]
        table = jnp.concatenate(
            screen + [inv_var, opacity] + colour + [jnp.zeros((1, HOME), F32)], axis=0
        )
        table = jnp.clip(table, -LARGE, LARGE)
        tab_send[which] = jnp.where(table == table, table, 0.0)

    lane = iota((1, LANES), 1)
    mine = isl_ref[me_c]
    offsets = jnp.concatenate([mine[0:1], mine[1:2], mine[0:1], mine[1:2]], axis=1)
    wanted = jnp.where(offsets >= 0, lax.rem(lane, CELLS) * OWN + offsets, -1)
    pick = (iota((ROWS, LANES), 0) == wanted).astype(F32).astype(BF16)
    all_ids = ids_ref[...]
    packed = jnp.concatenate(
        [
            (all_ids // LANES).astype(F32),
            lax.rem(all_ids, LANES).astype(F32),
            jnp.broadcast_to(cnt_ref[...].astype(F32), (16, ROWS)),
        ],
        axis=0,
    ).astype(BF16)
    picked = dot(packed, pick)
    left = iota((SUB, LANES), 1) < LISTS
    high = jnp.where(left, picked[0:8], picked[8:16])
    low = jnp.where(left, picked[16:24], picked[24:32])
    slot = iota((SUB, LANES), 0) + jnp.where(left, 0, SUB)
    live = slot.astype(F32) < picked[32:40]
    high = jnp.where(live, high, -1.0)
    hi_ref[...] = high
    for kk in range(SUB):
        hot = (iota((LANES, LANES), 0).astype(F32) == low[kk : kk + 1]).astype(F32).astype(BF16)
        for part in range(3):
            oh_ref[part * LANES : (part + 1) * LANES, kk * LANES : (kk + 1) * LANES] = hot

    both = jnp.concatenate([isl_ref[:, 0, :], isl_ref[:, 1, :]], axis=0).astype(F32)
    at_me = jnp.where(iota((LISTS, CELLS), 1) == me_c, both, 0.0)
    tile_half = jnp.sum(at_me, axis=1, keepdims=True)
    tile_col = jnp.concatenate([tile_half, tile_half], axis=0)
    eye = iota((LANES, LANES), 0) == iota((LANES, LANES), 1)
    tile_row = jnp.sum(jnp.where(eye, tile_col, 0.0), axis=0, keepdims=True)
    in_tile = (iota((OWN, LANES), 0).astype(F32) == tile_row).astype(F32)
    order = ord_ref[...].reshape(OWN, CELLS)
    cell_lane = lax.rem(iota((OWN, LANES), 1), CELLS)
    rank = jnp.zeros((OWN, LANES), F32)
    for at in range(CELLS):
        rank = jnp.where(order[:, at : at + 1] == cell_lane, float(at), rank)
    rank_row = jnp.sum(in_tile * rank, axis=0, keepdims=True)
    key_row = 2.0 * rank_row + jnp.where(lane < LISTS, 0.0, 1.0)
    key_col = jnp.sum(jnp.where(eye, key_row, 0.0), axis=1, keepdims=True)
    same = (tile_col == tile_row) & (tile_row >= 0.0)
    ahead = (same & (key_col < key_row)).astype(F32).astype(BF16)
    after = (same & (key_col > key_row)).astype(F32).astype(BF16)
    ahead3 = jnp.concatenate([ahead] * 3, axis=0)
    after2 = jnp.concatenate([after] * 2, axis=0)
    in_tile_b = in_tile.astype(BF16)
    in_tile3 = jnp.concatenate([in_tile_b] * 3, axis=1)
    in_tile2v = jnp.concatenate([in_tile_b] * 2, axis=0)
    tile_int = tile_row.astype(jnp.int32)
    window = lax.rem(me_v, HALF_VIEWS) * ROWS + me_c * OWN + tile_int
    side_at = iota((TSIDE, LANES), 0).astype(F32) + 0.5
    place_x = (lax.rem(window, 32) * TSIDE).astype(F32) + side_at
    place_y = ((window // 32) * TSIDE).astype(F32) + side_at
    acc_ref[...] = jnp.zeros_like(acc_ref)

    pl.semaphore_wait(barrier, VIEWS - 1 + CELLS - 1)

    def table_copy(d):
        to = peer_v(d)
        return pltpu.make_async_remote_copy(
            src_ref=tab_send.at[to // HALF_VIEWS],
            dst_ref=tab_recv.at[me_v],
            send_sem=sem_ts.at[d],
            recv_sem=sem_tr.at[me_v],
            device_id=(me_c, to),
            device_id_type=pl.DeviceIdType.MESH,
        )

    def table_start(d, carry):
        table_copy(d).start()
        return carry

    lax.fori_loop(1, VIEWS, table_start, 0)
    tab_recv[me_v] = tab_send[me_v // HALF_VIEWS]

    def table_wait(d, carry):
        pltpu.make_async_remote_copy(
            src_ref=tab_send.at[0],
            dst_ref=tab_recv.at[peer_v(d)],
            send_sem=sem_ts.at[d],
            recv_sem=sem_tr.at[peer_v(d)],
            device_id=(me_c, peer_v(d)),
            device_id_type=pl.DeviceIdType.MESH,
        ).wait_recv()
        return carry

    lax.fori_loop(1, VIEWS, table_wait, 0)

    blocks = []
    for home in range(VIEWS):
        for at in range(SUB):
            value = tab_recv[home, :, at * LANES : (at + 1) * LANES]
            blocks.append(value)
    parts = split3(jnp.concatenate(blocks, axis=0))
    lhs = jnp.concatenate(parts, axis=1)
    chosen = []
    for pair in range(4):
        got = dot(lhs, oh_ref[:, pair * 256 : (pair + 1) * 256])
        for side in range(2):
            hi = hi_ref[2 * pair + side : 2 * pair + side + 1, :]
            total = jnp.zeros((SUB, LANES), F32)
            for at in range(HIGHS):
                total = total + jnp.where(
                    hi == float(at), got[at * SUB : (at + 1) * SUB, side * LANES : (side + 1) * LANES], 0.0
                )
            chosen.append(total)
    lists = rows_to_lists(jnp.concatenate(chosen, axis=0))
    fwd_send[:, 0, :] = lists[:CELLS]
    fwd_send[:, 1, :] = lists[CELLS:]

    def cell_copy(source, target, sems, d):
        return pltpu.make_async_remote_copy(
            src_ref=source.at[peer_c(d)],
            dst_ref=target.at[me_c],
            send_sem=sems.at[0],
            recv_sem=sems.at[1],
            device_id=(peer_c(d), me_v),
            device_id_type=pl.DeviceIdType.MESH,
        )

    def cell_wait(buffer, sem):
        others = buffer.at[pl.ds(0, CELLS - 1)]
        pltpu.make_async_copy(others, others, sem).wait()

    def fwd_start(d, carry):
        cell_copy(fwd_send, fwd_recv, sem_f, d).start()
        return carry

    lax.fori_loop(1, CELLS, fwd_start, 0)
    fwd_recv[me_c] = fwd_send[me_c]

    cell_wait(fwd_recv, sem_f.at[1])
    v_ref[...] = lists_to_rows(
        jnp.concatenate([fwd_recv[:, 0, :], fwd_recv[:, 1, :]], axis=0)
    )

    def value(kk, j):
        return v_ref[kk * SUB + j : kk * SUB + j + 1, :]

    for kk in range(SUB):
        inv = -0.5 * value(kk, 2)
        dx = place_x - value(kk, 0)
        dy = place_y - value(kk, 1)
        ex_ref[kk] = value(kk, 3) * jnp.exp(inv * (dx * dx))
        ey_ref[kk] = jnp.exp(inv * (dy * dy))
        dy_ref[kk] = dy

    def forward(i, carry):
        rows = pl.ds(pl.multiple_of(i * 32, 32), 32)
        through = jnp.ones((32, LANES), F32)
        second = jnp.ones((32, LANES), F32)
        first = through
        sums = [jnp.zeros((32, LANES), F32) for ch in range(3)]
        for kk in range(SUB):
            ex = ex_ref[kk]
            alpha = jnp.concatenate(
                [ex * ey_ref[kk, pl.ds(2 * i + at, 1), :] for at in range(2)], axis=0
            )
            keep = 1.0 - alpha
            weight = alpha * through
            w_ref[kk, rows, :] = weight
            rho_ref[kk, rows, :] = alpha / keep
            for ch in range(3):
                sums[ch] = sums[ch] + weight * value(kk, 4 + ch)
            through = through * keep
            if kk < 4:
                first = through
            else:
                second = second * keep
        for ch in range(3):
            part_ref[ch, rows, :] = sums[ch]
        pre_ref[rows, :] = jnp.log(first) + jnp.log(second)
        return carry

    lax.fori_loop(0, 8, forward, 0)

    prefix = jnp.exp(dot(jnp.concatenate(split3(pre_ref[...]), axis=1), ahead3))
    pre_ref[...] = prefix
    owed = jnp.zeros((PIX, LANES), F32)
    for ch in range(3):
        seen = prefix * part_ref[ch]
        image = dot(in_tile3, jnp.concatenate(split3(seen), axis=1), ((1,), (1,)))
        rend_ref[pl.ds(2 * ch, OWN, stride=6), :] = image[:, :LANES]
        rend_ref[pl.ds(2 * ch + 1, OWN, stride=6), :] = image[:, LANES:]
        miss = image - tgt_ref[ch].astype(F32)
        miss2 = jnp.concatenate(split2(miss), axis=0)
        pulled = dot(miss2, in_tile2v, ((0,), (0,)))
        gl_ref[ch] = pulled
        owed = owed + seen * pulled
    behind_ref[...] = dot(jnp.concatenate(split2(owed), axis=1), after2)

    def backward(i, carry):
        rows = pl.ds(pl.multiple_of(i * 32, 32), 32)
        prefix = pre_ref[rows, :]
        behind = behind_ref[rows, :]
        pulled = [gl_ref[ch, rows, :] for ch in range(3)]
        for kk in reversed(range(SUB)):
            weight = prefix * w_ref[kk, rows, :]
            gain = (
                pulled[0] * value(kk, 4) + pulled[1] * value(kk, 5) + pulled[2] * value(kk, 6)
            )
            owed = weight * gain
            pull = owed - behind * rho_ref[kk, rows, :]
            behind = behind + owed
            up, down = pull[:16], pull[16:]
            dy_up = dy_ref[kk, pl.ds(2 * i, 1), :]
            dy_down = dy_ref[kk, pl.ds(2 * i + 1, 1), :]
            acc_ref[kk, 0] += up + down
            along = up * dy_up
            along_down = down * dy_down
            acc_ref[kk, 1] += along + along_down
            acc_ref[kk, 2] += along * dy_up + along_down * dy_down
            for ch in range(3):
                tint = weight * pulled[ch]
                acc_ref[kk, 3 + ch] += tint[:16] + tint[16:]
        return carry

    lax.fori_loop(0, 8, backward, 0)

    results = []
    for kk in range(SUB):
        dx = place_x - value(kk, 0)
        inv = value(kk, 2)
        base = acc_ref[kk, 0]
        base_x = base * dx

        def total(x):
            return jnp.sum(x, axis=0, keepdims=True)

        results += [
            inv * total(base_x),
            inv * total(acc_ref[kk, 1]),
            inv * total(base_x * dx + acc_ref[kk, 2]),
            (1.0 - value(kk, 3)) * total(base),
            total(acc_ref[kk, 3]),
            total(acc_ref[kk, 4]),
            total(acc_ref[kk, 5]),
            jnp.zeros((1, LANES), F32),
        ]
    lists = rows_to_lists(jnp.concatenate(results, axis=0))
    bwd_send[:, 0, :] = lists[:CELLS]
    bwd_send[:, 1, :] = lists[CELLS:]

    def bwd_start(d, carry):
        cell_copy(bwd_send, bwd_recv, sem_b, d).start()
        return carry

    lax.fori_loop(1, CELLS, bwd_start, 0)
    bwd_recv[me_c] = bwd_send[me_c]

    cell_wait(bwd_recv, sem_b.at[1])

    grads = lists_to_rows(jnp.concatenate([bwd_recv[:, 0, :], bwd_recv[:, 1, :]], axis=0))
    last = iota((SUB, LANES), 0) == SUB - 1
    for kk in range(SUB):
        hi = hi_ref[kk : kk + 1, :]
        piece = split2(jnp.where(last, 1.0, grads[kk * SUB : (kk + 1) * SUB]))
        piece = [x.astype(F32) for x in piece]
        for at in range(0, HIGHS, 2):
            here, there = hi == float(at), hi == float(at + 1)
            for part in range(2):
                lhs_ref[part, at * SUB : (at + 2) * SUB, kk * LANES : (kk + 1) * LANES] = (
                    jnp.concatenate(
                        [jnp.where(here, piece[part], 0.0), jnp.where(there, piece[part], 0.0)],
                        axis=0,
                    ).astype(BF16)
                )
    hot = oh_ref[0:LANES, :]
    spread = dot(lhs_ref[0], hot, ((1,), (1,)))
    spread = spread + dot(lhs_ref[1], hot, ((1,), (1,)))
    for home in range(VIEWS):
        for at in range(SUB):
            row = (home * SUB + at) * SUB
            grad_send[home, :, at * LANES : (at + 1) * LANES] = spread[row : row + SUB]

    def grad_start(d, carry):
        to = peer_v(d)
        pltpu.make_async_remote_copy(
            src_ref=grad_send.at[to],
            dst_ref=grad_recv.at[me_v],
            send_sem=sem_gs.at[d],
            recv_sem=sem_gr.at[me_v],
            device_id=(me_c, to),
            device_id_type=pl.DeviceIdType.MESH,
        ).start()
        return carry

    lax.fori_loop(1, VIEWS, grad_start, 0)
    grad_recv[me_v] = grad_send[me_v]

    def grad_arrived(d):
        return pltpu.make_async_remote_copy(
            src_ref=grad_send.at[peer_v(d)],
            dst_ref=grad_recv.at[peer_v(d)],
            send_sem=sem_gs.at[d],
            recv_sem=sem_gr.at[peer_v(d)],
            device_id=(me_c, peer_v(d)),
            device_id_type=pl.DeviceIdType.MESH,
        )

    def grad_wait(d, carry):
        grad_arrived(d).wait_recv()
        return carry

    lax.fori_loop(1, VIEWS, grad_wait, 0)
    gout_ref[0] = (grad_recv[0] + grad_recv[1]) + (grad_recv[2] + grad_recv[3])
    gout_ref[1] = (grad_recv[4] + grad_recv[5]) + (grad_recv[6] + grad_recv[7])

    def sent_view(d, carry):
        table_copy(d).wait_send()
        grad_arrived(d).wait_send()
        return carry

    for load in loads[7:]:
        load.wait()
    lax.fori_loop(1, VIEWS, sent_view, 0)
    cell_wait(fwd_send, sem_f.at[0])
    cell_wait(bwd_send, sem_b.at[0])


def adam_kernel(
    grad_ref,
    rend_ref,
    basis_ref,
    cam_ref,
    g_ref,
    one_ref,
    two_ref,
    rend_out,
    out_g,
    out_one,
    out_two,
    grads,
    new_g,
    new_one,
    new_two,
    sems,
):
    image = pltpu.make_async_copy(rend_ref, rend_out, sems.at[0, 0])
    image.start()
    touched = grad_ref[0, 7:8, :] + grad_ref[1, 7:8, :] > 0.5
    cameras = [camera_values(cam_ref, which) for which in range(2)]
    fix_one = 1.0 / (1.0 - beta_one**adam_step)
    fix_two = 1.0 / (1.0 - beta_two**adam_step)
    for k in range(3):
        grads[k : k + 1, :] = sum(
            cameras[which][row][k] * grad_ref[which, row : row + 1, :]
            for which in range(2)
            for row in range(2)
        )
    grads[3:5, :] = grad_ref[0, 2:4, :] + grad_ref[1, 2:4, :]
    columns = [basis_ref[which, :, 0:1] for which in range(2)]
    for ch in range(3):
        j = 4 + ch
        grads[5 + 16 * ch : 21 + 16 * ch, :] = (
            columns[0] * grad_ref[0, j : j + 1, :] + columns[1] * grad_ref[1, j : j + 1, :]
        )
    copies = [image]
    for at, (low, high) in enumerate(((0, 16), (16, 32), (32, 48), (48, 53))):
        rows = slice(low, high)
        grad = grads[rows, :]
        first = beta_one * one_ref[rows, :] + (1.0 - beta_one) * grad
        second = beta_two * two_ref[rows, :] + (1.0 - beta_two) * grad * grad
        change = learn_rate * (first * fix_one) / (jnp.sqrt(second * fix_two) + adam_eps)
        new_g[rows, :] = jnp.where(touched, g_ref[rows, :] - change, g_ref[rows, :])
        new_one[rows, :] = jnp.where(touched, first, one_ref[rows, :])
        new_two[rows, :] = jnp.where(touched, second, two_ref[rows, :])
        for which, (source, target) in enumerate(
            ((new_g, out_g), (new_one, out_one), (new_two, out_two))
        ):
            copy = pltpu.make_async_copy(
                source.at[pl.ds(low, high - low), :],
                target.at[pl.ds(low, high - low), :],
                sems.at[1 + at, which],
            )
            copy.start()
            copies.append(copy)
    for copy in copies:
        copy.wait()


def per_device(
    gaussians,
    moment_one,
    moment_two,
    cameras,
    target,
    gauss_ids,
    tile_counts,
    intersection_slots,
    depth_order,
):
    vmem = pl.BlockSpec(memory_space=pltpu.VMEM)
    hbm = pl.BlockSpec(memory_space=pltpu.HBM)
    shape = jax.ShapeDtypeStruct(gaussians.shape, F32)
    sems = pltpu.SemaphoreType.DMA
    rendered, grads, basis, cameras, gaussians, moment_one, moment_two = pl.pallas_call(
        step_kernel,
        out_shape=(
            jax.ShapeDtypeStruct((96, LANES), F32),
            jax.ShapeDtypeStruct((2, SUB, HOME), F32),
            jax.ShapeDtypeStruct((2, 16, LANES), F32),
            jax.ShapeDtypeStruct((2, 2, 4), F32),
            shape,
            shape,
            shape,
        ),
        in_specs=[hbm] * 9,
        out_specs=(vmem,) * 7,
        scratch_shapes=[
            pltpu.VMEM((3, OWN, PIX), BF16),
            pltpu.VMEM((16, ROWS), jnp.int32),
            pltpu.VMEM((1, ROWS), jnp.int32),
            pltpu.VMEM((CELLS, 2, CELLS), jnp.int32),
            pltpu.VMEM((OWN, 1, CELLS), jnp.int32),
            pltpu.VMEM((2, SUB, HOME), F32),
            pltpu.VMEM((VIEWS, SUB, HOME), F32),
            pltpu.VMEM((CELLS, 2, LANES), F32),
            pltpu.VMEM((CELLS, 2, LANES), F32),
            pltpu.VMEM((CELLS, 2, LANES), F32),
            pltpu.VMEM((CELLS, 2, LANES), F32),
            pltpu.VMEM((VIEWS, SUB, HOME), F32),
            pltpu.VMEM((VIEWS, SUB, HOME), F32),
            pltpu.VMEM((3 * LANES, SUB * LANES), BF16),
            pltpu.VMEM((SUB, LANES), F32),
            pltpu.VMEM((64, LANES), F32),
            pltpu.VMEM((SUB, TSIDE, LANES), F32),
            pltpu.VMEM((SUB, TSIDE, LANES), F32),
            pltpu.VMEM((SUB, TSIDE, LANES), F32),
            pltpu.VMEM((SUB, PIX, LANES), F32),
            pltpu.VMEM((SUB, PIX, LANES), F32),
            pltpu.VMEM((3, PIX, LANES), F32),
            pltpu.VMEM((PIX, LANES), F32),
            pltpu.VMEM((PIX, LANES), F32),
            pltpu.VMEM((3, PIX, LANES), F32),
            pltpu.VMEM((SUB, 6, TSIDE, LANES), F32),
            pltpu.VMEM((2, HIGHS * SUB, SUB * LANES), BF16),
            sems((VIEWS,)),
            sems((VIEWS,)),
            sems((2,)),
            sems((2,)),
            sems((VIEWS,)),
            sems((VIEWS,)),
            sems((9,)),
        ],
        compiler_params=pltpu.CompilerParams(
            collective_id=0, has_side_effects=True, vmem_limit_bytes=40 * 1024 * 1024
        ),
        name="splat_step",
    )(
        *(
            pltpu.with_memory_space_constraint(x, pltpu.HBM)
            for x in (
                gaussians,
                moment_one,
                moment_two,
                cameras,
                jnp.transpose(target[:, 0], (1, 0, 2)),
                jnp.transpose(gauss_ids[0, :, 0, :], (1, 0)),
                tile_counts.reshape(1, ROWS),
                jnp.transpose(intersection_slots[:, :, 0, :], (0, 2, 1)),
                depth_order,
            )
        )
    )
    image, new_gaussians, new_one, new_two = pl.pallas_call(
        adam_kernel,
        out_shape=(jax.ShapeDtypeStruct((96, LANES), F32), shape, shape, shape),
        in_specs=[vmem] * 7,
        out_specs=(hbm,) * 4,
        scratch_shapes=[
            pltpu.VMEM((56, HOME), F32),
            pltpu.VMEM(gaussians.shape, F32),
            pltpu.VMEM(gaussians.shape, F32),
            pltpu.VMEM(gaussians.shape, F32),
            sems((5, 3)),
        ],
        compiler_params=pltpu.CompilerParams(vmem_limit_bytes=20 * 1024 * 1024),
        name="adam",
    )(grads, rendered, basis, cameras, gaussians, moment_one, moment_two)
    return (image.reshape(OWN, 1, 3, PIX), new_gaussians, new_one, new_two)


def solution(mesh):
    placed = (
        P(None, ("cell", "view")),
        P(None, ("cell", "view")),
        P(None, ("cell", "view")),
        P(),
        P("cell", "view", None, None),
        P("cell", None, "view", None),
        P("cell", None, "view"),
        P(None, None, "view", None),
        P("cell", "view", None),
    )
    return jax.shard_map(
        per_device,
        mesh=mesh,
        in_specs=placed,
        out_specs=(
            P("cell", "view", None, None),
            P(None, ("cell", "view")),
            P(None, ("cell", "view")),
            P(None, ("cell", "view")),
        ),
        check_vma=False,
    )
```

```python
import jax
import jax.numpy as jnp
from jax import lax
from jax.experimental import pallas as pl
from jax.experimental.pallas import tpu as pltpu
from jax.sharding import PartitionSpec as P

CELLS = 32
VIEWS = 8
HALF_VIEWS = VIEWS // 2
HOME = 1024
OWN = 16
ROWS = 512
PIX = 256
TSIDE = 16
LISTS = 2 * CELLS
SUB = 8
LANES = 128
HIGHS = VIEWS * SUB
F32 = jnp.float32
BF16 = jnp.bfloat16
LARGE = 1e38

band_zero = 0.28209479177387814
band_one = 0.4886025119029199
band_two = (
    1.0925484305920792,
    -1.0925484305920792,
    0.31539156525252005,
    -1.0925484305920792,
    0.5462742152960396,
)
band_three = (
    -0.5900435899266435,
    2.890611442640554,
    -0.4570457994644658,
    0.3731763325901154,
    -0.4570457994644658,
    1.445305721320277,
    -0.5900435899266435,
)
beta_one = 0.9
beta_two = 0.999
learn_rate = 0.01
adam_eps = 1e-08
adam_step = 10.0


def iota(shape, axis):
    return lax.broadcasted_iota(jnp.int32, shape, axis)


def camera_values(cam_ref, which):
    return [[cam_ref[which, row : row + 1, k : k + 1] for k in range(4)] for row in range(2)]


def basis_column(camera):
    a, b = camera
    nx = a[1] * b[2] - a[2] * b[1]
    ny = a[2] * b[0] - a[0] * b[2]
    nz = a[0] * b[1] - a[1] * b[0]
    norm = jnp.sqrt(nx * nx + ny * ny + nz * nz)
    x, y, z = nx / norm, ny / norm, nz / norm
    xx, yy, zz = x * x, y * y, z * z
    terms = [
        x * 0.0 + band_zero,
        -band_one * y,
        band_one * z,
        -band_one * x,
        band_two[0] * x * y,
        band_two[1] * y * z,
        band_two[2] * (2.0 * zz - xx - yy),
        band_two[3] * x * z,
        band_two[4] * (xx - yy),
        band_three[0] * y * (3.0 * xx - yy),
        band_three[1] * x * y * z,
        band_three[2] * y * (4.0 * zz - xx - yy),
        band_three[3] * z * (2.0 * zz - 3.0 * xx - 3.0 * yy),
        band_three[4] * x * (4.0 * zz - xx - yy),
        band_three[5] * z * (xx - yy),
        band_three[6] * x * (xx - 3.0 * yy),
    ]
    row = iota((16, 1), 0)
    column = jnp.zeros((16, 1), F32)
    for at, term in enumerate(terms):
        column = jnp.where(row == at, term, column)
    return column


def split3(x):
    high = x.astype(BF16)
    rest = x - high.astype(F32)
    mid = rest.astype(BF16)
    low = (rest - mid.astype(F32)).astype(BF16)
    return high, mid, low


def split2(x):
    high = x.astype(BF16)
    return high, (x - high.astype(F32)).astype(BF16)


def dot(a, b, dims=((1,), (0,))):
    return lax.dot_general(a, b, (dims, ((), ())), preferred_element_type=F32)


def rows_to_lists(x):
    t = x.T
    return jnp.concatenate([t[:LISTS], t[LISTS:]], axis=1)


def lists_to_rows(x):
    t = x.T
    return jnp.concatenate([t[:64], t[64:]], axis=1)


def step_kernel(
    g_hbm,
    one_hbm,
    two_hbm,
    cam_hbm,
    tgt_hbm,
    ids_hbm,
    cnt_hbm,
    isl_hbm,
    ord_hbm,
    rend_ref,
    gout_ref,
    basis_ref,
    cam_ref,
    g_ref,
    one_ref,
    two_ref,
    tgt_ref,
    ids_ref,
    cnt_ref,
    isl_ref,
    ord_ref,
    tab_send,
    tab_recv,
    fwd_send,
    fwd_recv,
    bwd_send,
    bwd_recv,
    grad_send,
    grad_recv,
    oh_ref,
    hi_ref,
    v_ref,
    ex_ref,
    ey_ref,
    dy_ref,
    w_ref,
    rho_ref,
    part_ref,
    pre_ref,
    behind_ref,
    gl_ref,
    acc_ref,
    lhs_ref,
    sem_ts,
    sem_tr,
    sem_f,
    sem_b,
    sem_gs,
    sem_gr,
    sem_in,
    near_sem,
    line_sem,
):
    loads = [
        pltpu.make_async_copy(source, target, sem_in.at[at])
        for at, (source, target) in enumerate(
            (
                (g_hbm, g_ref),
                (cam_hbm, cam_ref),
                (isl_hbm, isl_ref),
                (ids_hbm, ids_ref),
                (cnt_hbm, cnt_ref),
                (ord_hbm, ord_ref),
                (tgt_hbm, tgt_ref),
                (one_hbm, one_ref),
                (two_hbm, two_ref),
            )
        )
    ]
    for load in loads[:7]:
        load.start()
    me_c = lax.axis_index("cell")
    me_v = lax.axis_index("view")

    def peer_c(d):
        return lax.rem(me_c + lax.rem(d + 10, CELLS - 1) + 1, CELLS)

    me_x, me_core = me_v // 2, lax.rem(me_v, 2)
    me_y, me_z = me_c // 8, lax.rem(me_c, 8)

    def chip_v(step):
        return 2 * lax.rem(me_x + step, 4)

    peers_v = [chip_v(step) + core for step in (2, 1, 3) for core in range(2)]
    peers_v.append(me_v + 1 - 2 * me_core)

    def near_z(d):
        return me_y * 8 + lax.rem(me_z + d + 1 + 3 * (d // 2), 8)

    def line_y(d):
        return lax.rem(me_y + d, 4) * 8 + me_z

    def signal(sem, cell):
        pl.semaphore_signal(
            sem, inc=1, device_id=(cell, me_v), device_id_type=pl.DeviceIdType.MESH
        )

    barrier = pltpu.get_barrier_semaphore()

    def greet_z(sem):
        def body(d, carry):
            signal(sem, near_z(d))
            return carry

        lax.fori_loop(0, 4, body, 0)

    def greet_y(sem):
        def body(d, carry):
            signal(sem, line_y(d))
            return carry

        lax.fori_loop(1, 4, body, 0)

    greet_z(barrier)
    greet_y(barrier)
    for peer in peers_v:
        pl.semaphore_signal(
            barrier, inc=1, device_id=(me_c, peer), device_id_type=pl.DeviceIdType.MESH
        )
    for load in loads[:7]:
        load.wait()
    for load in loads[7:]:
        load.start()

    centre = [g_ref[k : k + 1, :] for k in range(3)]
    inv_var = jnp.exp(-2.0 * g_ref[3:4, :])
    opacity = 1.0 / (1.0 + jnp.exp(-g_ref[4:5, :]))
    for which in range(2):
        camera = camera_values(cam_ref, which)
        column = basis_column(camera)
        basis_ref[which] = jnp.broadcast_to(column, (16, LANES))
        screen = [
            row[0] * centre[0] + row[1] * centre[1] + row[2] * centre[2] + row[3] for row in camera
        ]
        colour = [
            0.5 + jnp.sum(g_ref[5 + 16 * ch : 21 + 16 * ch, :] * column, axis=0, keepdims=True)
            for ch in range(3)
        ]
        table = jnp.concatenate(
            screen + [inv_var, opacity] + colour + [jnp.zeros((1, HOME), F32)], axis=0
        )
        table = jnp.clip(table, -LARGE, LARGE)
        tab_send[which] = jnp.where(table == table, table, 0.0)

    lane = iota((1, LANES), 1)
    mine = isl_ref[me_c]
    offsets = jnp.concatenate([mine[0:1], mine[1:2], mine[0:1], mine[1:2]], axis=1)
    wanted = jnp.where(offsets >= 0, lax.rem(lane, CELLS) * OWN + offsets, -1)
    pick = (iota((ROWS, LANES), 0) == wanted).astype(F32).astype(BF16)
    all_ids = ids_ref[...]
    packed = jnp.concatenate(
        [
            (all_ids // LANES).astype(F32),
            lax.rem(all_ids, LANES).astype(F32),
            jnp.broadcast_to(cnt_ref[...].astype(F32), (16, ROWS)),
        ],
        axis=0,
    ).astype(BF16)
    picked = dot(packed, pick)
    left = iota((SUB, LANES), 1) < LISTS
    high = jnp.where(left, picked[0:8], picked[8:16])
    low = jnp.where(left, picked[16:24], picked[24:32])
    slot = iota((SUB, LANES), 0) + jnp.where(left, 0, SUB)
    live = slot.astype(F32) < picked[32:40]
    high = jnp.where(live, high, -1.0)
    hi_ref[...] = high
    for kk in range(SUB):
        hot = (iota((LANES, LANES), 0).astype(F32) == low[kk : kk + 1]).astype(F32).astype(BF16)
        for part in range(3):
            oh_ref[part * LANES : (part + 1) * LANES, kk * LANES : (kk + 1) * LANES] = hot

    both = jnp.concatenate([isl_ref[:, 0, :], isl_ref[:, 1, :]], axis=0).astype(F32)
    at_me = jnp.where(iota((LISTS, CELLS), 1) == me_c, both, 0.0)
    tile_half = jnp.sum(at_me, axis=1, keepdims=True)
    tile_col = jnp.concatenate([tile_half, tile_half], axis=0)
    eye = iota((LANES, LANES), 0) == iota((LANES, LANES), 1)
    tile_row = jnp.sum(jnp.where(eye, tile_col, 0.0), axis=0, keepdims=True)
    in_tile = (iota((OWN, LANES), 0).astype(F32) == tile_row).astype(F32)
    order = ord_ref[...].reshape(OWN, CELLS)
    cell_lane = lax.rem(iota((OWN, LANES), 1), CELLS)
    rank = jnp.zeros((OWN, LANES), F32)
    for at in range(CELLS):
        rank = jnp.where(order[:, at : at + 1] == cell_lane, float(at), rank)
    rank_row = jnp.sum(in_tile * rank, axis=0, keepdims=True)
    key_row = 2.0 * rank_row + jnp.where(lane < LISTS, 0.0, 1.0)
    key_col = jnp.sum(jnp.where(eye, key_row, 0.0), axis=1, keepdims=True)
    same = (tile_col == tile_row) & (tile_row >= 0.0)
    ahead = (same & (key_col < key_row)).astype(F32).astype(BF16)
    after = (same & (key_col > key_row)).astype(F32).astype(BF16)
    ahead3 = jnp.concatenate([ahead] * 3, axis=0)
    after2 = jnp.concatenate([after] * 2, axis=0)
    in_tile_b = in_tile.astype(BF16)
    in_tile3 = jnp.concatenate([in_tile_b] * 3, axis=1)
    in_tile2v = jnp.concatenate([in_tile_b] * 2, axis=0)
    tile_int = tile_row.astype(jnp.int32)
    window = lax.rem(me_v, HALF_VIEWS) * ROWS + me_c * OWN + tile_int
    side_at = iota((TSIDE, LANES), 0).astype(F32) + 0.5
    place_x = (lax.rem(window, 32) * TSIDE).astype(F32) + side_at
    place_y = ((window // 32) * TSIDE).astype(F32) + side_at
    acc_ref[...] = jnp.zeros_like(acc_ref)

    pl.semaphore_wait(barrier, VIEWS - 1 + 7)
    greet_z(near_sem)
    greet_y(near_sem)

    def table_copy(at):
        to = peers_v[at]
        return pltpu.make_async_remote_copy(
            src_ref=tab_send.at[to // HALF_VIEWS],
            dst_ref=tab_recv.at[me_v],
            send_sem=sem_ts.at[at],
            recv_sem=sem_tr.at[me_v],
            device_id=(me_c, to),
            device_id_type=pl.DeviceIdType.MESH,
        )

    def table_wait(at):
        pltpu.make_async_remote_copy(
            src_ref=tab_send.at[0],
            dst_ref=tab_recv.at[peers_v[at]],
            send_sem=sem_ts.at[at],
            recv_sem=sem_tr.at[peers_v[at]],
            device_id=(me_c, peers_v[at]),
            device_id_type=pl.DeviceIdType.MESH,
        ).wait_recv()

    for at in range(VIEWS - 1):
        table_copy(at).start()
    tab_recv[me_v] = tab_send[me_v // HALF_VIEWS]

    chosen = [jnp.zeros((SUB, LANES), F32) for kk in range(SUB)]
    for group, (steps, arrivals) in enumerate((((0,), (6,)), ((1, 3), (2, 3, 4, 5)), ((2,), (0, 1)))):
        for at in arrivals:
            table_wait(at)
        if group == 0:
            pl.semaphore_wait(near_sem, 7)
            greet_y(line_sem)
        blocks, highs = [], []
        for step in steps:
            for core in range(2):
                home = chip_v(step) + core
                for at in range(SUB):
                    blocks.append(tab_recv[home, :, at * LANES : (at + 1) * LANES])
                    highs.append((home * SUB + at).astype(F32))
        lhs = jnp.concatenate(split3(jnp.concatenate(blocks, axis=0)), axis=1)
        for pair in range(4):
            got = dot(lhs, oh_ref[:, pair * 256 : (pair + 1) * 256])
            for side in range(2):
                kk = 2 * pair + side
                hi = hi_ref[kk : kk + 1, :]
                for at, value_at in enumerate(highs):
                    chosen[kk] = chosen[kk] + jnp.where(
                        hi == value_at,
                        got[at * SUB : (at + 1) * SUB, side * LANES : (side + 1) * LANES],
                        0.0,
                    )
    lists = rows_to_lists(jnp.concatenate(chosen, axis=0))
    fwd_send[:, 0, :] = lists[:CELLS]
    fwd_send[:, 1, :] = lists[CELLS:]

    def cell_copy(source, target, sems, d):
        return pltpu.make_async_remote_copy(
            src_ref=source.at[peer_c(d)],
            dst_ref=target.at[me_c],
            send_sem=sems.at[0],
            recv_sem=sems.at[1],
            device_id=(peer_c(d), me_v),
            device_id_type=pl.DeviceIdType.MESH,
        )

    def cell_wait(buffer, sem):
        others = buffer.at[pl.ds(0, CELLS - 1)]
        pltpu.make_async_copy(others, others, sem).wait()

    def fwd_start(d, carry):
        cell_copy(fwd_send, fwd_recv, sem_f, d).start()
        return carry

    pl.semaphore_wait(line_sem, 3)
    lax.fori_loop(1, CELLS, fwd_start, 0)
    fwd_recv[me_c] = fwd_send[me_c]

    cell_wait(fwd_recv, sem_f.at[1])
    v_ref[...] = lists_to_rows(
        jnp.concatenate([fwd_recv[:, 0, :], fwd_recv[:, 1, :]], axis=0)
    )

    def value(kk, j):
        return v_ref[kk * SUB + j : kk * SUB + j + 1, :]

    for kk in range(SUB):
        inv = -0.5 * value(kk, 2)
        dx = place_x - value(kk, 0)
        dy = place_y - value(kk, 1)
        ex_ref[kk] = value(kk, 3) * jnp.exp(inv * (dx * dx))
        ey_ref[kk] = jnp.exp(inv * (dy * dy))
        dy_ref[kk] = dy

    def forward(i, carry):
        rows = pl.ds(pl.multiple_of(i * 32, 32), 32)
        through = jnp.ones((32, LANES), F32)
        second = jnp.ones((32, LANES), F32)
        first = through
        sums = [jnp.zeros((32, LANES), F32) for ch in range(3)]
        for kk in range(SUB):
            ex = ex_ref[kk]
            alpha = jnp.concatenate(
                [ex * ey_ref[kk, pl.ds(2 * i + at, 1), :] for at in range(2)], axis=0
            )
            keep = 1.0 - alpha
            weight = alpha * through
            w_ref[kk, rows, :] = weight
            rho_ref[kk, rows, :] = alpha / keep
            for ch in range(3):
                sums[ch] = sums[ch] + weight * value(kk, 4 + ch)
            through = through * keep
            if kk < 4:
                first = through
            else:
                second = second * keep
        for ch in range(3):
            part_ref[ch, rows, :] = sums[ch]
        pre_ref[rows, :] = jnp.log(first) + jnp.log(second)
        return carry

    lax.fori_loop(0, 8, forward, 0)

    prefix = jnp.exp(dot(jnp.concatenate(split3(pre_ref[...]), axis=1), ahead3))
    pre_ref[...] = prefix
    owed = jnp.zeros((PIX, LANES), F32)
    for ch in range(3):
        seen = prefix * part_ref[ch]
        image = dot(in_tile3, jnp.concatenate(split3(seen), axis=1), ((1,), (1,)))
        rend_ref[pl.ds(2 * ch, OWN, stride=6), :] = image[:, :LANES]
        rend_ref[pl.ds(2 * ch + 1, OWN, stride=6), :] = image[:, LANES:]
        miss = image - tgt_ref[ch].astype(F32)
        miss2 = jnp.concatenate(split2(miss), axis=0)
        pulled = dot(miss2, in_tile2v, ((0,), (0,)))
        gl_ref[ch] = pulled
        owed = owed + seen * pulled
    behind_ref[...] = dot(jnp.concatenate(split2(owed), axis=1), after2)

    def backward(i, carry):
        rows = pl.ds(pl.multiple_of(i * 32, 32), 32)
        prefix = pre_ref[rows, :]
        behind = behind_ref[rows, :]
        pulled = [gl_ref[ch, rows, :] for ch in range(3)]
        for kk in reversed(range(SUB)):
            weight = prefix * w_ref[kk, rows, :]
            gain = (
                pulled[0] * value(kk, 4) + pulled[1] * value(kk, 5) + pulled[2] * value(kk, 6)
            )
            owed = weight * gain
            pull = owed - behind * rho_ref[kk, rows, :]
            behind = behind + owed
            up, down = pull[:16], pull[16:]
            dy_up = dy_ref[kk, pl.ds(2 * i, 1), :]
            dy_down = dy_ref[kk, pl.ds(2 * i + 1, 1), :]
            acc_ref[kk, 0] += up + down
            along = up * dy_up
            along_down = down * dy_down
            acc_ref[kk, 1] += along + along_down
            acc_ref[kk, 2] += along * dy_up + along_down * dy_down
            for ch in range(3):
                tint = weight * pulled[ch]
                acc_ref[kk, 3 + ch] += tint[:16] + tint[16:]
        return carry

    lax.fori_loop(0, 8, backward, 0)

    results = []
    for kk in range(SUB):
        dx = place_x - value(kk, 0)
        inv = value(kk, 2)
        base = acc_ref[kk, 0]
        base_x = base * dx

        def total(x):
            return jnp.sum(x, axis=0, keepdims=True)

        results += [
            inv * total(base_x),
            inv * total(acc_ref[kk, 1]),
            inv * total(base_x * dx + acc_ref[kk, 2]),
            (1.0 - value(kk, 3)) * total(base),
            total(acc_ref[kk, 3]),
            total(acc_ref[kk, 4]),
            total(acc_ref[kk, 5]),
            jnp.zeros((1, LANES), F32),
        ]
    lists = rows_to_lists(jnp.concatenate(results, axis=0))
    bwd_send[:, 0, :] = lists[:CELLS]
    bwd_send[:, 1, :] = lists[CELLS:]

    def bwd_start(d, carry):
        cell_copy(bwd_send, bwd_recv, sem_b, d).start()
        return carry

    lax.fori_loop(1, CELLS, bwd_start, 0)
    bwd_recv[me_c] = bwd_send[me_c]

    cell_wait(bwd_recv, sem_b.at[1])

    grads = lists_to_rows(jnp.concatenate([bwd_recv[:, 0, :], bwd_recv[:, 1, :]], axis=0))
    last = iota((SUB, LANES), 0) == SUB - 1
    pieces = []
    for kk in range(SUB):
        piece = split2(jnp.where(last, 1.0, grads[kk * SUB : (kk + 1) * SUB]))
        pieces.append([x.astype(F32) for x in piece])
    hot = oh_ref[0:LANES, :]

    def grad_copy(at):
        return pltpu.make_async_remote_copy(
            src_ref=grad_send.at[peers_v[at]],
            dst_ref=grad_recv.at[me_v],
            send_sem=sem_gs.at[at],
            recv_sem=sem_gr.at[me_v],
            device_id=(me_c, peers_v[at]),
            device_id_type=pl.DeviceIdType.MESH,
        )

    def grad_arrived(at):
        return pltpu.make_async_remote_copy(
            src_ref=grad_send.at[peers_v[at]],
            dst_ref=grad_recv.at[peers_v[at]],
            send_sem=sem_gs.at[at],
            recv_sem=sem_gr.at[peers_v[at]],
            device_id=(me_c, peers_v[at]),
            device_id_type=pl.DeviceIdType.MESH,
        )

    for steps, sends in (((2,), (0, 1)), ((1, 3), (2, 3, 4, 5)), ((0,), (6,))):
        homes = [chip_v(step) + core for step in steps for core in range(2)]
        count = len(homes) * SUB
        for kk in range(SUB):
            hi = hi_ref[kk : kk + 1, :]
            for at in range(0, count, 2):
                first = (homes[at // SUB] * SUB + at % SUB).astype(F32)
                here, there = hi == first, hi == first + 1.0
                for part in range(2):
                    lhs_ref[part, at * SUB : (at + 2) * SUB, kk * LANES : (kk + 1) * LANES] = (
                        jnp.concatenate(
                            [
                                jnp.where(here, pieces[kk][part], 0.0),
                                jnp.where(there, pieces[kk][part], 0.0),
                            ],
                            axis=0,
                        ).astype(BF16)
                    )
        rows = slice(0, count * SUB)
        spread = dot(lhs_ref[0, rows, :], hot, ((1,), (1,)))
        spread = spread + dot(lhs_ref[1, rows, :], hot, ((1,), (1,)))
        for which, home in enumerate(homes):
            for at in range(SUB):
                row = (which * SUB + at) * SUB
                grad_send[home, :, at * LANES : (at + 1) * LANES] = spread[row : row + SUB]
        for at in sends:
            grad_copy(at).start()
    grad_recv[me_v] = grad_send[me_v]
    for at in range(VIEWS - 1):
        grad_arrived(at).wait_recv()
    gout_ref[0] = (grad_recv[0] + grad_recv[1]) + (grad_recv[2] + grad_recv[3])
    gout_ref[1] = (grad_recv[4] + grad_recv[5]) + (grad_recv[6] + grad_recv[7])

    for load in loads[7:]:
        load.wait()
    for at in range(VIEWS - 1):
        table_copy(at).wait_send()
        grad_copy(at).wait_send()
    cell_wait(fwd_send, sem_f.at[0])
    cell_wait(bwd_send, sem_b.at[0])


def adam_kernel(
    grad_ref,
    rend_ref,
    basis_ref,
    cam_ref,
    g_ref,
    one_ref,
    two_ref,
    rend_out,
    out_g,
    out_one,
    out_two,
    grads,
    new_g,
    new_one,
    new_two,
    sems,
):
    image = pltpu.make_async_copy(rend_ref, rend_out, sems.at[0, 0])
    image.start()
    touched = grad_ref[0, 7:8, :] + grad_ref[1, 7:8, :] > 0.5
    cameras = [camera_values(cam_ref, which) for which in range(2)]
    fix_one = 1.0 / (1.0 - beta_one**adam_step)
    fix_two = 1.0 / (1.0 - beta_two**adam_step)
    for k in range(3):
        grads[k : k + 1, :] = sum(
            cameras[which][row][k] * grad_ref[which, row : row + 1, :]
            for which in range(2)
            for row in range(2)
        )
    grads[3:5, :] = grad_ref[0, 2:4, :] + grad_ref[1, 2:4, :]
    columns = [basis_ref[which, :, 0:1] for which in range(2)]
    for ch in range(3):
        j = 4 + ch
        grads[5 + 16 * ch : 21 + 16 * ch, :] = (
            columns[0] * grad_ref[0, j : j + 1, :] + columns[1] * grad_ref[1, j : j + 1, :]
        )
    copies = [image]
    for at, (low, high) in enumerate(((0, 16), (16, 32), (32, 48), (48, 53))):
        rows = slice(low, high)
        grad = grads[rows, :]
        first = beta_one * one_ref[rows, :] + (1.0 - beta_one) * grad
        second = beta_two * two_ref[rows, :] + (1.0 - beta_two) * grad * grad
        change = learn_rate * (first * fix_one) / (jnp.sqrt(second * fix_two) + adam_eps)
        new_g[rows, :] = jnp.where(touched, g_ref[rows, :] - change, g_ref[rows, :])
        new_one[rows, :] = jnp.where(touched, first, one_ref[rows, :])
        new_two[rows, :] = jnp.where(touched, second, two_ref[rows, :])
        for which, (source, target) in enumerate(
            ((new_g, out_g), (new_one, out_one), (new_two, out_two))
        ):
            copy = pltpu.make_async_copy(
                source.at[pl.ds(low, high - low), :],
                target.at[pl.ds(low, high - low), :],
                sems.at[1 + at, which],
            )
            copy.start()
            copies.append(copy)
    for copy in copies:
        copy.wait()


def per_device(
    gaussians,
    moment_one,
    moment_two,
    cameras,
    target,
    gauss_ids,
    tile_counts,
    intersection_slots,
    depth_order,
):
    vmem = pl.BlockSpec(memory_space=pltpu.VMEM)
    hbm = pl.BlockSpec(memory_space=pltpu.HBM)
    shape = jax.ShapeDtypeStruct(gaussians.shape, F32)
    sems = pltpu.SemaphoreType.DMA
    rendered, grads, basis, cameras, gaussians, moment_one, moment_two = pl.pallas_call(
        step_kernel,
        out_shape=(
            jax.ShapeDtypeStruct((96, LANES), F32),
            jax.ShapeDtypeStruct((2, SUB, HOME), F32),
            jax.ShapeDtypeStruct((2, 16, LANES), F32),
            jax.ShapeDtypeStruct((2, 2, 4), F32),
            shape,
            shape,
            shape,
        ),
        in_specs=[hbm] * 9,
        out_specs=(vmem,) * 7,
        scratch_shapes=[
            pltpu.VMEM((3, OWN, PIX), BF16),
            pltpu.VMEM((16, ROWS), jnp.int32),
            pltpu.VMEM((1, ROWS), jnp.int32),
            pltpu.VMEM((CELLS, 2, CELLS), jnp.int32),
            pltpu.VMEM((OWN, 1, CELLS), jnp.int32),
            pltpu.VMEM((2, SUB, HOME), F32),
            pltpu.VMEM((VIEWS, SUB, HOME), F32),
            pltpu.VMEM((CELLS, 2, LANES), F32),
            pltpu.VMEM((CELLS, 2, LANES), F32),
            pltpu.VMEM((CELLS, 2, LANES), F32),
            pltpu.VMEM((CELLS, 2, LANES), F32),
            pltpu.VMEM((VIEWS, SUB, HOME), F32),
            pltpu.VMEM((VIEWS, SUB, HOME), F32),
            pltpu.VMEM((3 * LANES, SUB * LANES), BF16),
            pltpu.VMEM((SUB, LANES), F32),
            pltpu.VMEM((64, LANES), F32),
            pltpu.VMEM((SUB, TSIDE, LANES), F32),
            pltpu.VMEM((SUB, TSIDE, LANES), F32),
            pltpu.VMEM((SUB, TSIDE, LANES), F32),
            pltpu.VMEM((SUB, PIX, LANES), F32),
            pltpu.VMEM((SUB, PIX, LANES), F32),
            pltpu.VMEM((3, PIX, LANES), F32),
            pltpu.VMEM((PIX, LANES), F32),
            pltpu.VMEM((PIX, LANES), F32),
            pltpu.VMEM((3, PIX, LANES), F32),
            pltpu.VMEM((SUB, 6, TSIDE, LANES), F32),
            pltpu.VMEM((2, HIGHS * SUB // 2, SUB * LANES), BF16),
            sems((VIEWS,)),
            sems((VIEWS,)),
            sems((2,)),
            sems((2,)),
            sems((VIEWS,)),
            sems((VIEWS,)),
            sems((9,)),
            pltpu.SemaphoreType.REGULAR,
            pltpu.SemaphoreType.REGULAR,
        ],
        compiler_params=pltpu.CompilerParams(
            collective_id=0, has_side_effects=True, vmem_limit_bytes=40 * 1024 * 1024
        ),
        name="splat_step",
    )(
        *(
            pltpu.with_memory_space_constraint(x, pltpu.HBM)
            for x in (
                gaussians,
                moment_one,
                moment_two,
                cameras,
                jnp.transpose(target[:, 0], (1, 0, 2)),
                jnp.transpose(gauss_ids[0, :, 0, :], (1, 0)),
                tile_counts.reshape(1, ROWS),
                jnp.transpose(intersection_slots[:, :, 0, :], (0, 2, 1)),
                depth_order,
            )
        )
    )
    image, new_gaussians, new_one, new_two = pl.pallas_call(
        adam_kernel,
        out_shape=(jax.ShapeDtypeStruct((96, LANES), F32), shape, shape, shape),
        in_specs=[vmem] * 7,
        out_specs=(hbm,) * 4,
        scratch_shapes=[
            pltpu.VMEM((56, HOME), F32),
            pltpu.VMEM(gaussians.shape, F32),
            pltpu.VMEM(gaussians.shape, F32),
            pltpu.VMEM(gaussians.shape, F32),
            sems((5, 3)),
        ],
        compiler_params=pltpu.CompilerParams(vmem_limit_bytes=20 * 1024 * 1024),
        name="adam",
    )(grads, rendered, basis, cameras, gaussians, moment_one, moment_two)
    return (image.reshape(OWN, 1, 3, PIX), new_gaussians, new_one, new_two)


def solution(mesh):
    placed = (
        P(None, ("cell", "view")),
        P(None, ("cell", "view")),
        P(None, ("cell", "view")),
        P(),
        P("cell", "view", None, None),
        P("cell", None, "view", None),
        P("cell", None, "view"),
        P(None, None, "view", None),
        P("cell", "view", None),
    )
    return jax.shard_map(
        per_device,
        mesh=mesh,
        in_specs=placed,
        out_specs=(
            P("cell", "view", None, None),
            P(None, ("cell", "view")),
            P(None, ("cell", "view")),
            P(None, ("cell", "view")),
        ),
        check_vma=False,
    )
```

```python
import jax
import jax.numpy as jnp
from jax import lax
from jax.experimental import pallas as pl
from jax.experimental.pallas import tpu as pltpu
from jax.sharding import PartitionSpec as P

CELLS = 32
VIEWS = 8
HALF_VIEWS = VIEWS // 2
HOME = 1024
OWN = 16
ROWS = 512
PIX = 256
TSIDE = 16
LISTS = 2 * CELLS
SUB = 8
LANES = 128
HIGHS = VIEWS * SUB
F32 = jnp.float32
BF16 = jnp.bfloat16
LARGE = 1e38

band_zero = 0.28209479177387814
band_one = 0.4886025119029199
band_two = (
    1.0925484305920792,
    -1.0925484305920792,
    0.31539156525252005,
    -1.0925484305920792,
    0.5462742152960396,
)
band_three = (
    -0.5900435899266435,
    2.890611442640554,
    -0.4570457994644658,
    0.3731763325901154,
    -0.4570457994644658,
    1.445305721320277,
    -0.5900435899266435,
)
beta_one = 0.9
beta_two = 0.999
learn_rate = 0.01
adam_eps = 1e-08
adam_step = 10.0


def iota(shape, axis):
    return lax.broadcasted_iota(jnp.int32, shape, axis)


def camera_values(cam_ref, which):
    return [[cam_ref[which, row : row + 1, k : k + 1] for k in range(4)] for row in range(2)]


def basis_column(camera):
    a, b = camera
    nx = a[1] * b[2] - a[2] * b[1]
    ny = a[2] * b[0] - a[0] * b[2]
    nz = a[0] * b[1] - a[1] * b[0]
    norm = jnp.sqrt(nx * nx + ny * ny + nz * nz)
    x, y, z = nx / norm, ny / norm, nz / norm
    xx, yy, zz = x * x, y * y, z * z
    terms = [
        x * 0.0 + band_zero,
        -band_one * y,
        band_one * z,
        -band_one * x,
        band_two[0] * x * y,
        band_two[1] * y * z,
        band_two[2] * (2.0 * zz - xx - yy),
        band_two[3] * x * z,
        band_two[4] * (xx - yy),
        band_three[0] * y * (3.0 * xx - yy),
        band_three[1] * x * y * z,
        band_three[2] * y * (4.0 * zz - xx - yy),
        band_three[3] * z * (2.0 * zz - 3.0 * xx - 3.0 * yy),
        band_three[4] * x * (4.0 * zz - xx - yy),
        band_three[5] * z * (xx - yy),
        band_three[6] * x * (xx - 3.0 * yy),
    ]
    row = iota((16, 1), 0)
    column = jnp.zeros((16, 1), F32)
    for at, term in enumerate(terms):
        column = jnp.where(row == at, term, column)
    return column


def split3(x):
    high = x.astype(BF16)
    rest = x - high.astype(F32)
    mid = rest.astype(BF16)
    low = (rest - mid.astype(F32)).astype(BF16)
    return high, mid, low


def split2(x):
    high = x.astype(BF16)
    return high, (x - high.astype(F32)).astype(BF16)


def dot(a, b, dims=((1,), (0,))):
    return lax.dot_general(a, b, (dims, ((), ())), preferred_element_type=F32)


def rows_to_lists(x):
    t = x.T
    return jnp.concatenate([t[:LISTS], t[LISTS:]], axis=1)


def lists_to_rows(x):
    t = x.T
    return jnp.concatenate([t[:64], t[64:]], axis=1)


def step_kernel(
    g_hbm,
    one_hbm,
    two_hbm,
    cam_hbm,
    tgt_hbm,
    ids_hbm,
    cnt_hbm,
    isl_hbm,
    ord_hbm,
    rend_ref,
    gout_ref,
    basis_ref,
    cam_ref,
    g_ref,
    one_ref,
    two_ref,
    tgt_ref,
    ids_ref,
    cnt_ref,
    isl_ref,
    ord_ref,
    tab_send,
    tab_recv,
    fwd_send,
    fwd_recv,
    bwd_send,
    bwd_recv,
    grad_send,
    grad_recv,
    oh_ref,
    hi_ref,
    v_ref,
    ex_ref,
    ey_ref,
    dy_ref,
    w_ref,
    rho_ref,
    part_ref,
    pre_ref,
    behind_ref,
    gl_ref,
    acc_ref,
    sum_ref,
    lhs_ref,
    sem_ts,
    sem_tr,
    sem_f,
    sem_b,
    sem_gs,
    sem_gr,
    sem_in,
    near_sem,
    line_sem,
):
    loads = [
        pltpu.make_async_copy(source, target, sem_in.at[at])
        for at, (source, target) in enumerate(
            (
                (g_hbm, g_ref),
                (cam_hbm, cam_ref),
                (isl_hbm, isl_ref),
                (ids_hbm, ids_ref),
                (cnt_hbm, cnt_ref),
                (ord_hbm, ord_ref),
                (tgt_hbm, tgt_ref),
                (one_hbm, one_ref),
                (two_hbm, two_ref),
            )
        )
    ]
    for load in loads[:7]:
        load.start()
    me_c = lax.axis_index("cell")
    me_v = lax.axis_index("view")

    def peer_c(d):
        return lax.rem(me_c + lax.rem(d + 10, CELLS - 1) + 1, CELLS)

    me_x, me_core = me_v // 2, lax.rem(me_v, 2)
    me_y, me_z = me_c // 8, lax.rem(me_c, 8)

    def chip_v(step):
        return 2 * lax.rem(me_x + step, 4)

    peers_v = [chip_v(step) + core for step in (2, 1, 3) for core in range(2)]
    peers_v.append(me_v + 1 - 2 * me_core)

    def near_z(d):
        return me_y * 8 + lax.rem(me_z + d + 1 + 3 * (d // 2), 8)

    def line_y(d):
        return lax.rem(me_y + d, 4) * 8 + me_z

    def signal(sem, cell):
        pl.semaphore_signal(
            sem, inc=1, device_id=(cell, me_v), device_id_type=pl.DeviceIdType.MESH
        )

    barrier = pltpu.get_barrier_semaphore()

    def greet_z(sem):
        def body(d, carry):
            signal(sem, near_z(d))
            return carry

        lax.fori_loop(0, 4, body, 0)

    def greet_y(sem):
        def body(d, carry):
            signal(sem, line_y(d))
            return carry

        lax.fori_loop(1, 4, body, 0)

    greet_z(barrier)
    greet_y(barrier)
    for peer in peers_v:
        pl.semaphore_signal(
            barrier, inc=1, device_id=(me_c, peer), device_id_type=pl.DeviceIdType.MESH
        )
    for load in loads[:7]:
        load.wait()
    for load in loads[7:]:
        load.start()

    centre = [g_ref[k : k + 1, :] for k in range(3)]
    inv_var = jnp.exp(-2.0 * g_ref[3:4, :])
    opacity = 1.0 / (1.0 + jnp.exp(-g_ref[4:5, :]))
    for which in range(2):
        camera = camera_values(cam_ref, which)
        column = basis_column(camera)
        basis_ref[which] = jnp.broadcast_to(column, (16, LANES))
        screen = [
            row[0] * centre[0] + row[1] * centre[1] + row[2] * centre[2] + row[3] for row in camera
        ]
        colour = [
            0.5 + jnp.sum(g_ref[5 + 16 * ch : 21 + 16 * ch, :] * column, axis=0, keepdims=True)
            for ch in range(3)
        ]
        table = jnp.concatenate(
            screen + [inv_var, opacity] + colour + [jnp.zeros((1, HOME), F32)], axis=0
        )
        table = jnp.clip(table, -LARGE, LARGE)
        tab_send[which] = jnp.where(table == table, table, 0.0)

    lane = iota((1, LANES), 1)
    mine = isl_ref[me_c]
    offsets = jnp.concatenate([mine[0:1], mine[1:2], mine[0:1], mine[1:2]], axis=1)
    wanted = jnp.where(offsets >= 0, lax.rem(lane, CELLS) * OWN + offsets, -1)
    pick = (iota((ROWS, LANES), 0) == wanted).astype(F32).astype(BF16)
    all_ids = ids_ref[...]
    packed = jnp.concatenate(
        [
            (all_ids // LANES).astype(F32),
            lax.rem(all_ids, LANES).astype(F32),
            jnp.broadcast_to(cnt_ref[...].astype(F32), (16, ROWS)),
        ],
        axis=0,
    ).astype(BF16)
    picked = dot(packed, pick)
    left = iota((SUB, LANES), 1) < LISTS
    high = jnp.where(left, picked[0:8], picked[8:16])
    low = jnp.where(left, picked[16:24], picked[24:32])
    slot = iota((SUB, LANES), 0) + jnp.where(left, 0, SUB)
    live = slot.astype(F32) < picked[32:40]
    high = jnp.where(live, high, -1.0)
    hi_ref[...] = high
    for kk in range(SUB):
        hot = (iota((LANES, LANES), 0).astype(F32) == low[kk : kk + 1]).astype(F32).astype(BF16)
        for part in range(3):
            oh_ref[part * LANES : (part + 1) * LANES, kk * LANES : (kk + 1) * LANES] = hot

    both = jnp.concatenate([isl_ref[:, 0, :], isl_ref[:, 1, :]], axis=0).astype(F32)
    at_me = jnp.where(iota((LISTS, CELLS), 1) == me_c, both, 0.0)
    tile_half = jnp.sum(at_me, axis=1, keepdims=True)
    tile_col = jnp.concatenate([tile_half, tile_half], axis=0)
    eye = iota((LANES, LANES), 0) == iota((LANES, LANES), 1)
    tile_row = jnp.sum(jnp.where(eye, tile_col, 0.0), axis=0, keepdims=True)
    in_tile = (iota((OWN, LANES), 0).astype(F32) == tile_row).astype(F32)
    order = ord_ref[...].reshape(OWN, CELLS)
    cell_lane = lax.rem(iota((OWN, LANES), 1), CELLS)
    rank = jnp.zeros((OWN, LANES), F32)
    for at in range(CELLS):
        rank = jnp.where(order[:, at : at + 1] == cell_lane, float(at), rank)
    rank_row = jnp.sum(in_tile * rank, axis=0, keepdims=True)
    key_row = 2.0 * rank_row + jnp.where(lane < LISTS, 0.0, 1.0)
    key_col = jnp.sum(jnp.where(eye, key_row, 0.0), axis=1, keepdims=True)
    same = (tile_col == tile_row) & (tile_row >= 0.0)
    ahead = (same & (key_col < key_row)).astype(F32).astype(BF16)
    after = (same & (key_col > key_row)).astype(F32).astype(BF16)
    ahead2 = jnp.concatenate([ahead] * 2, axis=0)
    after2 = jnp.concatenate([after] * 2, axis=0)
    in_tile_b = in_tile.astype(BF16)
    in_tile2 = jnp.concatenate([in_tile_b] * 2, axis=1)
    in_tile2v = jnp.concatenate([in_tile_b] * 2, axis=0)
    tile_int = tile_row.astype(jnp.int32)
    window = lax.rem(me_v, HALF_VIEWS) * ROWS + me_c * OWN + tile_int
    side_at = iota((TSIDE, LANES), 0).astype(F32) + 0.5
    place_x = (lax.rem(window, 32) * TSIDE).astype(F32) + side_at
    place_y = ((window // 32) * TSIDE).astype(F32) + side_at
    acc_ref[...] = jnp.zeros_like(acc_ref)
    sum_ref[...] = jnp.zeros_like(sum_ref)

    pl.semaphore_wait(barrier, VIEWS - 1 + 7)
    signal(near_sem, near_z(1))
    signal(near_sem, near_z(2))

    def table_copy(at):
        to = peers_v[at]
        return pltpu.make_async_remote_copy(
            src_ref=tab_send.at[to // HALF_VIEWS],
            dst_ref=tab_recv.at[me_v],
            send_sem=sem_ts.at[at],
            recv_sem=sem_tr.at[me_v],
            device_id=(me_c, to),
            device_id_type=pl.DeviceIdType.MESH,
        )

    def table_wait(at):
        pltpu.make_async_remote_copy(
            src_ref=tab_send.at[0],
            dst_ref=tab_recv.at[peers_v[at]],
            send_sem=sem_ts.at[at],
            recv_sem=sem_tr.at[peers_v[at]],
            device_id=(me_c, peers_v[at]),
            device_id_type=pl.DeviceIdType.MESH,
        ).wait_recv()

    for at in range(VIEWS - 1):
        table_copy(at).start()
    tab_recv[me_v] = tab_send[me_v // HALF_VIEWS]

    chosen = [jnp.zeros((SUB, LANES), F32) for kk in range(SUB)]
    for group, (steps, arrivals) in enumerate((((0,), (6,)), ((1, 3), (2, 3, 4, 5)), ((2,), (0, 1)))):
        for at in arrivals:
            table_wait(at)
        if group == 0:
            pl.semaphore_wait(near_sem, 2)
            greet_y(line_sem)
        blocks, highs = [], []
        for step in steps:
            for core in range(2):
                home = chip_v(step) + core
                for at in range(SUB):
                    blocks.append(tab_recv[home, :, at * LANES : (at + 1) * LANES])
                    highs.append((home * SUB + at).astype(F32))
        lhs = jnp.concatenate(split3(jnp.concatenate(blocks, axis=0)), axis=1)
        for pair in range(4):
            got = dot(lhs, oh_ref[:, pair * 256 : (pair + 1) * 256])
            for side in range(2):
                kk = 2 * pair + side
                hi = hi_ref[kk : kk + 1, :]
                for at, value_at in enumerate(highs):
                    chosen[kk] = chosen[kk] + jnp.where(
                        hi == value_at,
                        got[at * SUB : (at + 1) * SUB, side * LANES : (side + 1) * LANES],
                        0.0,
                    )
    lists = rows_to_lists(jnp.concatenate(chosen, axis=0))
    fwd_send[:, 0, :] = lists[:CELLS]
    fwd_send[:, 1, :] = lists[CELLS:]

    def cell_copy(source, target, sems, d):
        return pltpu.make_async_remote_copy(
            src_ref=source.at[peer_c(d)],
            dst_ref=target.at[me_c],
            send_sem=sems.at[0],
            recv_sem=sems.at[1],
            device_id=(peer_c(d), me_v),
            device_id_type=pl.DeviceIdType.MESH,
        )

    def cell_wait(buffer, sem):
        others = buffer.at[pl.ds(0, CELLS - 1)]
        pltpu.make_async_copy(others, others, sem).wait()

    def fwd_start(d, carry):
        cell_copy(fwd_send, fwd_recv, sem_f, d).start()
        return carry

    pl.semaphore_wait(line_sem, 3)
    lax.fori_loop(1, CELLS, fwd_start, 0)
    fwd_recv[me_c] = fwd_send[me_c]

    cell_wait(fwd_recv, sem_f.at[1])
    v_ref[...] = lists_to_rows(
        jnp.concatenate([fwd_recv[:, 0, :], fwd_recv[:, 1, :]], axis=0)
    )

    def value(kk, j):
        return v_ref[kk * SUB + j : kk * SUB + j + 1, :]

    for kk in range(SUB):
        inv = -0.5 * value(kk, 2)
        dx = place_x - value(kk, 0)
        dy = place_y - value(kk, 1)
        ex_ref[kk] = value(kk, 3) * jnp.exp(inv * (dx * dx))
        ey_ref[kk] = jnp.exp(inv * (dy * dy))
        dy_ref[kk] = dy

    def forward(i, carry):
        rows = pl.ds(pl.multiple_of(i * 32, 32), 32)
        through = jnp.ones((32, LANES), F32)
        second = jnp.ones((32, LANES), F32)
        first = through
        sums = [jnp.zeros((32, LANES), F32) for ch in range(3)]
        for kk in range(SUB):
            ex = ex_ref[kk]
            alpha = jnp.concatenate(
                [ex * ey_ref[kk, pl.ds(2 * i + at, 1), :] for at in range(2)], axis=0
            )
            keep = 1.0 - alpha
            weight = alpha * through
            w_ref[kk, rows, :] = weight
            inverse = pl.reciprocal(keep, approx=True)
            rho_ref[kk, rows, :] = alpha * (inverse * (2.0 - keep * inverse))
            for ch in range(3):
                sums[ch] = sums[ch] + weight * value(kk, 4 + ch)
            through = through * keep
            if kk < 4:
                first = through
            else:
                second = second * keep
        for ch in range(3):
            part_ref[ch, rows, :] = sums[ch]
        pre_ref[rows, :] = jnp.log(first) + jnp.log(second)
        return carry

    lax.fori_loop(0, 8, forward, 0)

    prefix = jnp.exp(dot(jnp.concatenate(split2(pre_ref[...]), axis=1), ahead2))
    pre_ref[...] = prefix
    owed = jnp.zeros((PIX, LANES), F32)
    for ch in range(3):
        seen = prefix * part_ref[ch]
        image = dot(in_tile2, jnp.concatenate(split2(seen), axis=1), ((1,), (1,)))
        rend_ref[pl.ds(2 * ch, OWN, stride=6), :] = image[:, :LANES]
        rend_ref[pl.ds(2 * ch + 1, OWN, stride=6), :] = image[:, LANES:]
        miss = image - tgt_ref[ch].astype(F32)
        miss2 = jnp.concatenate(split2(miss), axis=0)
        pulled = dot(miss2, in_tile2v, ((0,), (0,)))
        gl_ref[ch] = pulled
        owed = owed + seen * pulled
    behind_ref[...] = dot(jnp.concatenate(split2(owed), axis=1), after2)

    def backward(i, carry):
        rows = pl.ds(pl.multiple_of(i * 32, 32), 32)
        prefix = pre_ref[rows, :]
        behind = behind_ref[rows, :]
        pulled = [gl_ref[ch, rows, :] for ch in range(3)]
        for kk in reversed(range(SUB)):
            weight = prefix * w_ref[kk, rows, :]
            tints = [weight * pulled[ch] for ch in range(3)]
            owed = tints[0] * value(kk, 4) + tints[1] * value(kk, 5) + tints[2] * value(kk, 6)
            pull = owed - behind * rho_ref[kk, rows, :]
            behind = behind + owed
            up, down = pull[:16], pull[16:]
            acc_ref[kk] += up + down
            dy_up = dy_ref[kk, pl.ds(2 * i, 1), :]
            dy_down = dy_ref[kk, pl.ds(2 * i + 1, 1), :]
            along_up = (up[:8] + up[8:]) * dy_up
            along_down = (down[:8] + down[8:]) * dy_down
            sum_ref[kk, 0] += along_up + along_down
            sum_ref[kk, 1] += along_up * dy_up + along_down * dy_down
            for ch in range(3):
                tint = tints[ch]
                sum_ref[kk, 2 + ch] += (tint[:8] + tint[8:16]) + (tint[16:24] + tint[24:])
        return carry

    lax.fori_loop(0, 8, backward, 0)

    results = []
    for kk in range(SUB):
        dx = place_x - value(kk, 0)
        inv = value(kk, 2)
        base = acc_ref[kk]
        base_x = base * dx
        base_xx = base_x * dx

        def total(x):
            return jnp.sum(x, axis=0, keepdims=True)

        results += [
            inv * total(base_x),
            inv * total(sum_ref[kk, 0]),
            inv * total((base_xx[:8] + base_xx[8:]) + sum_ref[kk, 1]),
            (1.0 - value(kk, 3)) * total(base),
            total(sum_ref[kk, 2]),
            total(sum_ref[kk, 3]),
            total(sum_ref[kk, 4]),
            jnp.zeros((1, LANES), F32),
        ]
    lists = rows_to_lists(jnp.concatenate(results, axis=0))
    bwd_send[:, 0, :] = lists[:CELLS]
    bwd_send[:, 1, :] = lists[CELLS:]

    def bwd_start(d, carry):
        cell_copy(bwd_send, bwd_recv, sem_b, d).start()
        return carry

    lax.fori_loop(1, CELLS, bwd_start, 0)
    bwd_recv[me_c] = bwd_send[me_c]

    cell_wait(bwd_recv, sem_b.at[1])

    grads = lists_to_rows(jnp.concatenate([bwd_recv[:, 0, :], bwd_recv[:, 1, :]], axis=0))
    last = iota((SUB, LANES), 0) == SUB - 1
    pieces = []
    for kk in range(SUB):
        piece = split2(jnp.where(last, 1.0, grads[kk * SUB : (kk + 1) * SUB]))
        pieces.append([x.astype(F32) for x in piece])
    hot = oh_ref[0:LANES, :]

    def grad_copy(at):
        return pltpu.make_async_remote_copy(
            src_ref=grad_send.at[peers_v[at]],
            dst_ref=grad_recv.at[me_v],
            send_sem=sem_gs.at[at],
            recv_sem=sem_gr.at[me_v],
            device_id=(me_c, peers_v[at]),
            device_id_type=pl.DeviceIdType.MESH,
        )

    def grad_arrived(at):
        return pltpu.make_async_remote_copy(
            src_ref=grad_send.at[peers_v[at]],
            dst_ref=grad_recv.at[peers_v[at]],
            send_sem=sem_gs.at[at],
            recv_sem=sem_gr.at[peers_v[at]],
            device_id=(me_c, peers_v[at]),
            device_id_type=pl.DeviceIdType.MESH,
        )

    for steps, sends in (((2,), (0, 1)), ((1, 3), (2, 3, 4, 5)), ((0,), (6,))):
        homes = [chip_v(step) + core for step in steps for core in range(2)]
        count = len(homes) * SUB
        for kk in range(SUB):
            hi = hi_ref[kk : kk + 1, :]
            for at in range(0, count, 2):
                first = (homes[at // SUB] * SUB + at % SUB).astype(F32)
                here, there = hi == first, hi == first + 1.0
                for part in range(2):
                    lhs_ref[part, at * SUB : (at + 2) * SUB, kk * LANES : (kk + 1) * LANES] = (
                        jnp.concatenate(
                            [
                                jnp.where(here, pieces[kk][part], 0.0),
                                jnp.where(there, pieces[kk][part], 0.0),
                            ],
                            axis=0,
                        ).astype(BF16)
                    )
        rows = slice(0, count * SUB)
        spread = dot(lhs_ref[0, rows, :], hot, ((1,), (1,)))
        spread = spread + dot(lhs_ref[1, rows, :], hot, ((1,), (1,)))
        for which, home in enumerate(homes):
            for at in range(SUB):
                row = (which * SUB + at) * SUB
                grad_send[home, :, at * LANES : (at + 1) * LANES] = spread[row : row + SUB]
        for at in sends:
            grad_copy(at).start()
    grad_recv[me_v] = grad_send[me_v]
    for at in range(VIEWS - 1):
        grad_arrived(at).wait_recv()
    gout_ref[0] = (grad_recv[0] + grad_recv[1]) + (grad_recv[2] + grad_recv[3])
    gout_ref[1] = (grad_recv[4] + grad_recv[5]) + (grad_recv[6] + grad_recv[7])

    for load in loads[7:]:
        load.wait()
    for at in range(VIEWS - 1):
        table_copy(at).wait_send()
        grad_copy(at).wait_send()
    cell_wait(fwd_send, sem_f.at[0])
    cell_wait(bwd_send, sem_b.at[0])


def adam_kernel(
    grad_ref,
    rend_ref,
    basis_ref,
    cam_ref,
    g_ref,
    one_ref,
    two_ref,
    rend_out,
    out_g,
    out_one,
    out_two,
    grads,
    new_g,
    new_one,
    new_two,
    sems,
):
    image = pltpu.make_async_copy(rend_ref, rend_out, sems.at[0, 0])
    image.start()
    touched = grad_ref[0, 7:8, :] + grad_ref[1, 7:8, :] > 0.5
    cameras = [camera_values(cam_ref, which) for which in range(2)]
    fix_one = 1.0 / (1.0 - beta_one**adam_step)
    fix_two = 1.0 / (1.0 - beta_two**adam_step)
    for k in range(3):
        grads[k : k + 1, :] = sum(
            cameras[which][row][k] * grad_ref[which, row : row + 1, :]
            for which in range(2)
            for row in range(2)
        )
    grads[3:5, :] = grad_ref[0, 2:4, :] + grad_ref[1, 2:4, :]
    columns = [basis_ref[which, :, 0:1] for which in range(2)]
    for ch in range(3):
        j = 4 + ch
        grads[5 + 16 * ch : 21 + 16 * ch, :] = (
            columns[0] * grad_ref[0, j : j + 1, :] + columns[1] * grad_ref[1, j : j + 1, :]
        )
    copies = [image]
    for at, (low, high) in enumerate(((0, 16), (16, 32), (32, 48), (48, 53))):
        rows = slice(low, high)
        grad = grads[rows, :]
        first = beta_one * one_ref[rows, :] + (1.0 - beta_one) * grad
        second = beta_two * two_ref[rows, :] + (1.0 - beta_two) * grad * grad
        change = learn_rate * (first * fix_one) / (jnp.sqrt(second * fix_two) + adam_eps)
        new_g[rows, :] = jnp.where(touched, g_ref[rows, :] - change, g_ref[rows, :])
        new_one[rows, :] = jnp.where(touched, first, one_ref[rows, :])
        new_two[rows, :] = jnp.where(touched, second, two_ref[rows, :])
        for which, (source, target) in enumerate(
            ((new_g, out_g), (new_one, out_one), (new_two, out_two))
        ):
            copy = pltpu.make_async_copy(
                source.at[pl.ds(low, high - low), :],
                target.at[pl.ds(low, high - low), :],
                sems.at[1 + at, which],
            )
            copy.start()
            copies.append(copy)
    for copy in copies:
        copy.wait()


def per_device(
    gaussians,
    moment_one,
    moment_two,
    cameras,
    target,
    gauss_ids,
    tile_counts,
    intersection_slots,
    depth_order,
):
    vmem = pl.BlockSpec(memory_space=pltpu.VMEM)
    hbm = pl.BlockSpec(memory_space=pltpu.HBM)
    shape = jax.ShapeDtypeStruct(gaussians.shape, F32)
    sems = pltpu.SemaphoreType.DMA
    rendered, grads, basis, cameras, gaussians, moment_one, moment_two = pl.pallas_call(
        step_kernel,
        out_shape=(
            jax.ShapeDtypeStruct((96, LANES), F32),
            jax.ShapeDtypeStruct((2, SUB, HOME), F32),
            jax.ShapeDtypeStruct((2, 16, LANES), F32),
            jax.ShapeDtypeStruct((2, 2, 4), F32),
            shape,
            shape,
            shape,
        ),
        in_specs=[hbm] * 9,
        out_specs=(vmem,) * 7,
        scratch_shapes=[
            pltpu.VMEM((3, OWN, PIX), BF16),
            pltpu.VMEM((16, ROWS), jnp.int32),
            pltpu.VMEM((1, ROWS), jnp.int32),
            pltpu.VMEM((CELLS, 2, CELLS), jnp.int32),
            pltpu.VMEM((OWN, 1, CELLS), jnp.int32),
            pltpu.VMEM((2, SUB, HOME), F32),
            pltpu.VMEM((VIEWS, SUB, HOME), F32),
            pltpu.VMEM((CELLS, 2, LANES), F32),
            pltpu.VMEM((CELLS, 2, LANES), F32),
            pltpu.VMEM((CELLS, 2, LANES), F32),
            pltpu.VMEM((CELLS, 2, LANES), F32),
            pltpu.VMEM((VIEWS, SUB, HOME), F32),
            pltpu.VMEM((VIEWS, SUB, HOME), F32),
            pltpu.VMEM((3 * LANES, SUB * LANES), BF16),
            pltpu.VMEM((SUB, LANES), F32),
            pltpu.VMEM((64, LANES), F32),
            pltpu.VMEM((SUB, TSIDE, LANES), F32),
            pltpu.VMEM((SUB, TSIDE, LANES), F32),
            pltpu.VMEM((SUB, TSIDE, LANES), F32),
            pltpu.VMEM((SUB, PIX, LANES), F32),
            pltpu.VMEM((SUB, PIX, LANES), F32),
            pltpu.VMEM((3, PIX, LANES), F32),
            pltpu.VMEM((PIX, LANES), F32),
            pltpu.VMEM((PIX, LANES), F32),
            pltpu.VMEM((3, PIX, LANES), F32),
            pltpu.VMEM((SUB, TSIDE, LANES), F32),
            pltpu.VMEM((SUB, 5, SUB, LANES), F32),
            pltpu.VMEM((2, HIGHS * SUB // 2, SUB * LANES), BF16),
            sems((VIEWS,)),
            sems((VIEWS,)),
            sems((2,)),
            sems((2,)),
            sems((VIEWS,)),
            sems((VIEWS,)),
            sems((9,)),
            pltpu.SemaphoreType.REGULAR,
            pltpu.SemaphoreType.REGULAR,
        ],
        compiler_params=pltpu.CompilerParams(
            collective_id=0, has_side_effects=True, vmem_limit_bytes=40 * 1024 * 1024
        ),
        name="splat_step",
    )(
        *(
            pltpu.with_memory_space_constraint(x, pltpu.HBM)
            for x in (
                gaussians,
                moment_one,
                moment_two,
                cameras,
                jnp.transpose(target[:, 0], (1, 0, 2)),
                jnp.transpose(gauss_ids[0, :, 0, :], (1, 0)),
                tile_counts.reshape(1, ROWS),
                jnp.transpose(intersection_slots[:, :, 0, :], (0, 2, 1)),
                depth_order,
            )
        )
    )
    image, new_gaussians, new_one, new_two = pl.pallas_call(
        adam_kernel,
        out_shape=(jax.ShapeDtypeStruct((96, LANES), F32), shape, shape, shape),
        in_specs=[vmem] * 7,
        out_specs=(hbm,) * 4,
        scratch_shapes=[
            pltpu.VMEM((56, HOME), F32),
            pltpu.VMEM(gaussians.shape, F32),
            pltpu.VMEM(gaussians.shape, F32),
            pltpu.VMEM(gaussians.shape, F32),
            sems((5, 3)),
        ],
        compiler_params=pltpu.CompilerParams(vmem_limit_bytes=20 * 1024 * 1024),
        name="adam",
    )(grads, rendered, basis, cameras, gaussians, moment_one, moment_two)
    return (image.reshape(OWN, 1, 3, PIX), new_gaussians, new_one, new_two)


def solution(mesh):
    placed = (
        P(None, ("cell", "view")),
        P(None, ("cell", "view")),
        P(None, ("cell", "view")),
        P(),
        P("cell", "view", None, None),
        P("cell", None, "view", None),
        P("cell", None, "view"),
        P(None, None, "view", None),
        P("cell", "view", None),
    )
    return jax.shard_map(
        per_device,
        mesh=mesh,
        in_specs=placed,
        out_specs=(
            P("cell", "view", None, None),
            P(None, ("cell", "view")),
            P(None, ("cell", "view")),
            P(None, ("cell", "view")),
        ),
        check_vma=False,
    )
```

```python
import jax
import jax.numpy as jnp
from jax import lax
from jax.experimental import pallas as pl
from jax.experimental.pallas import tpu as pltpu
from jax.sharding import PartitionSpec as P

CELLS = 32
VIEWS = 8
HALF_VIEWS = VIEWS // 2
HOME = 1024
OWN = 16
ROWS = 512
PIX = 256
TSIDE = 16
LISTS = 2 * CELLS
SUB = 8
LANES = 128
HIGHS = VIEWS * SUB
F32 = jnp.float32
BF16 = jnp.bfloat16
LARGE = 1e38

band_zero = 0.28209479177387814
band_one = 0.4886025119029199
band_two = (
    1.0925484305920792,
    -1.0925484305920792,
    0.31539156525252005,
    -1.0925484305920792,
    0.5462742152960396,
)
band_three = (
    -0.5900435899266435,
    2.890611442640554,
    -0.4570457994644658,
    0.3731763325901154,
    -0.4570457994644658,
    1.445305721320277,
    -0.5900435899266435,
)
beta_one = 0.9
beta_two = 0.999
learn_rate = 0.01
adam_eps = 1e-08
adam_step = 10.0


def iota(shape, axis):
    return lax.broadcasted_iota(jnp.int32, shape, axis)


def camera_values(cam_ref, which):
    return [[cam_ref[which, row : row + 1, k : k + 1] for k in range(4)] for row in range(2)]


def basis_column(camera):
    a, b = camera
    nx = a[1] * b[2] - a[2] * b[1]
    ny = a[2] * b[0] - a[0] * b[2]
    nz = a[0] * b[1] - a[1] * b[0]
    norm = jnp.sqrt(nx * nx + ny * ny + nz * nz)
    x, y, z = nx / norm, ny / norm, nz / norm
    xx, yy, zz = x * x, y * y, z * z
    terms = [
        x * 0.0 + band_zero,
        -band_one * y,
        band_one * z,
        -band_one * x,
        band_two[0] * x * y,
        band_two[1] * y * z,
        band_two[2] * (2.0 * zz - xx - yy),
        band_two[3] * x * z,
        band_two[4] * (xx - yy),
        band_three[0] * y * (3.0 * xx - yy),
        band_three[1] * x * y * z,
        band_three[2] * y * (4.0 * zz - xx - yy),
        band_three[3] * z * (2.0 * zz - 3.0 * xx - 3.0 * yy),
        band_three[4] * x * (4.0 * zz - xx - yy),
        band_three[5] * z * (xx - yy),
        band_three[6] * x * (xx - 3.0 * yy),
    ]
    row = iota((16, 1), 0)
    column = jnp.zeros((16, 1), F32)
    for at, term in enumerate(terms):
        column = jnp.where(row == at, term, column)
    return column


def split3(x):
    high = x.astype(BF16)
    rest = x - high.astype(F32)
    mid = rest.astype(BF16)
    low = (rest - mid.astype(F32)).astype(BF16)
    return high, mid, low


def split2(x):
    high = x.astype(BF16)
    return high, (x - high.astype(F32)).astype(BF16)


def dot(a, b, dims=((1,), (0,))):
    return lax.dot_general(a, b, (dims, ((), ())), preferred_element_type=F32)


def rows_to_lists(x):
    t = x.T
    return jnp.concatenate([t[:LISTS], t[LISTS:]], axis=1)


def lists_to_rows(x):
    t = x.T
    return jnp.concatenate([t[:64], t[64:]], axis=1)


def step_kernel(
    g_hbm,
    one_hbm,
    two_hbm,
    cam_hbm,
    tgt_hbm,
    ids_hbm,
    cnt_hbm,
    isl_hbm,
    ord_hbm,
    rend_ref,
    gout_ref,
    basis_ref,
    cam_ref,
    g_ref,
    one_ref,
    two_ref,
    tgt_ref,
    ids_ref,
    cnt_ref,
    isl_ref,
    ord_ref,
    tab_send,
    tab_recv,
    fwd_send,
    fwd_recv,
    bwd_send,
    bwd_recv,
    grad_send,
    grad_recv,
    oh_ref,
    hi_ref,
    v_ref,
    ex_ref,
    ey_ref,
    dy_ref,
    w_ref,
    rho_ref,
    part_ref,
    pre_ref,
    behind_ref,
    gl_ref,
    acc_ref,
    sum_ref,
    lhs_ref,
    sem_ts,
    sem_tr,
    sem_f,
    sem_b,
    sem_gs,
    sem_gr,
    sem_in,
    near_sem,
    line_sem,
):
    loads = [
        pltpu.make_async_copy(source, target, sem_in.at[at])
        for at, (source, target) in enumerate(
            (
                (g_hbm, g_ref),
                (cam_hbm, cam_ref),
                (isl_hbm, isl_ref),
                (ids_hbm, ids_ref),
                (cnt_hbm, cnt_ref),
                (ord_hbm, ord_ref),
                (tgt_hbm, tgt_ref),
                (one_hbm, one_ref),
                (two_hbm, two_ref),
            )
        )
    ]
    for load in loads[:7]:
        load.start()
    me_c = lax.axis_index("cell")
    me_v = lax.axis_index("view")

    def peer_c(d):
        return lax.rem(me_c + lax.rem(d + 10, CELLS - 1) + 1, CELLS)

    me_x, me_core = me_v // 2, lax.rem(me_v, 2)
    me_y, me_z = me_c // 8, lax.rem(me_c, 8)

    def chip_v(step):
        return 2 * lax.rem(me_x + step, 4)

    peers_v = [chip_v(step) + core for step in (2, 1, 3) for core in range(2)]
    peers_v.append(me_v + 1 - 2 * me_core)

    def near_z(d):
        return me_y * 8 + lax.rem(me_z + d + 1 + 3 * (d // 2), 8)

    def line_y(d):
        return lax.rem(me_y + d, 4) * 8 + me_z

    def signal(sem, cell):
        pl.semaphore_signal(
            sem, inc=1, device_id=(cell, me_v), device_id_type=pl.DeviceIdType.MESH
        )

    barrier = pltpu.get_barrier_semaphore()

    def greet_z(sem):
        def body(d, carry):
            signal(sem, near_z(d))
            return carry

        lax.fori_loop(0, 4, body, 0)

    def greet_y(sem):
        def body(d, carry):
            signal(sem, line_y(d))
            return carry

        lax.fori_loop(1, 4, body, 0)

    greet_z(barrier)
    greet_y(barrier)
    for peer in peers_v:
        pl.semaphore_signal(
            barrier, inc=1, device_id=(me_c, peer), device_id_type=pl.DeviceIdType.MESH
        )
    for load in loads[:7]:
        load.wait()
    for load in loads[7:]:
        load.start()

    centre = [g_ref[k : k + 1, :] for k in range(3)]
    inv_var = jnp.exp(-2.0 * g_ref[3:4, :])
    opacity = 1.0 / (1.0 + jnp.exp(-g_ref[4:5, :]))
    for which in range(2):
        camera = camera_values(cam_ref, which)
        column = basis_column(camera)
        basis_ref[which] = jnp.broadcast_to(column, (16, LANES))
        screen = [
            row[0] * centre[0] + row[1] * centre[1] + row[2] * centre[2] + row[3] for row in camera
        ]
        colour = [
            0.5 + jnp.sum(g_ref[5 + 16 * ch : 21 + 16 * ch, :] * column, axis=0, keepdims=True)
            for ch in range(3)
        ]
        table = jnp.concatenate(
            screen + [inv_var, opacity] + colour + [jnp.zeros((1, HOME), F32)], axis=0
        )
        table = jnp.clip(table, -LARGE, LARGE)
        tab_send[which] = jnp.where(table == table, table, 0.0)

    lane = iota((1, LANES), 1)
    mine = isl_ref[me_c]
    offsets = jnp.concatenate([mine[0:1], mine[1:2], mine[0:1], mine[1:2]], axis=1)
    wanted = jnp.where(offsets >= 0, lax.rem(lane, CELLS) * OWN + offsets, -1)
    pick = (iota((ROWS, LANES), 0) == wanted).astype(F32).astype(BF16)
    all_ids = ids_ref[...]
    packed = jnp.concatenate(
        [
            (all_ids // LANES).astype(F32),
            lax.rem(all_ids, LANES).astype(F32),
            jnp.broadcast_to(cnt_ref[...].astype(F32), (16, ROWS)),
        ],
        axis=0,
    ).astype(BF16)
    picked = dot(packed, pick)
    left = iota((SUB, LANES), 1) < LISTS
    high = jnp.where(left, picked[0:8], picked[8:16])
    low = jnp.where(left, picked[16:24], picked[24:32])
    slot = iota((SUB, LANES), 0) + jnp.where(left, 0, SUB)
    live = slot.astype(F32) < picked[32:40]
    high = jnp.where(live, high, -1.0)
    hi_ref[...] = high
    for kk in range(SUB):
        hot = (iota((LANES, LANES), 0).astype(F32) == low[kk : kk + 1]).astype(F32).astype(BF16)
        for part in range(3):
            oh_ref[part * LANES : (part + 1) * LANES, kk * LANES : (kk + 1) * LANES] = hot

    pl.semaphore_wait(barrier, VIEWS - 1 + 7)
    signal(near_sem, near_z(1))
    signal(near_sem, near_z(2))

    def table_copy(at):
        to = peers_v[at]
        return pltpu.make_async_remote_copy(
            src_ref=tab_send.at[to // HALF_VIEWS],
            dst_ref=tab_recv.at[me_v],
            send_sem=sem_ts.at[at],
            recv_sem=sem_tr.at[me_v],
            device_id=(me_c, to),
            device_id_type=pl.DeviceIdType.MESH,
        )

    def table_wait(at):
        pltpu.make_async_remote_copy(
            src_ref=tab_send.at[0],
            dst_ref=tab_recv.at[peers_v[at]],
            send_sem=sem_ts.at[at],
            recv_sem=sem_tr.at[peers_v[at]],
            device_id=(me_c, peers_v[at]),
            device_id_type=pl.DeviceIdType.MESH,
        ).wait_recv()

    for at in range(VIEWS - 1):
        table_copy(at).start()
    tab_recv[me_v] = tab_send[me_v // HALF_VIEWS]

    chosen = [jnp.zeros((SUB, LANES), F32) for kk in range(SUB)]
    for group, (steps, arrivals) in enumerate((((0,), (6,)), ((1, 3), (2, 3, 4, 5)), ((2,), (0, 1)))):
        for at in arrivals:
            table_wait(at)
        if group == 0:
            pl.semaphore_wait(near_sem, 2)
            greet_y(line_sem)
        blocks, highs = [], []
        for step in steps:
            for core in range(2):
                home = chip_v(step) + core
                for at in range(SUB):
                    blocks.append(tab_recv[home, :, at * LANES : (at + 1) * LANES])
                    highs.append((home * SUB + at).astype(F32))
        lhs = jnp.concatenate(split3(jnp.concatenate(blocks, axis=0)), axis=1)
        for pair in range(4):
            got = dot(lhs, oh_ref[:, pair * 256 : (pair + 1) * 256])
            for side in range(2):
                kk = 2 * pair + side
                hi = hi_ref[kk : kk + 1, :]
                for at, value_at in enumerate(highs):
                    chosen[kk] = chosen[kk] + jnp.where(
                        hi == value_at,
                        got[at * SUB : (at + 1) * SUB, side * LANES : (side + 1) * LANES],
                        0.0,
                    )
    lists = rows_to_lists(jnp.concatenate(chosen, axis=0))
    fwd_send[:, 0, :] = lists[:CELLS]
    fwd_send[:, 1, :] = lists[CELLS:]

    def cell_copy(source, target, sems, d):
        return pltpu.make_async_remote_copy(
            src_ref=source.at[peer_c(d)],
            dst_ref=target.at[me_c],
            send_sem=sems.at[0],
            recv_sem=sems.at[1],
            device_id=(peer_c(d), me_v),
            device_id_type=pl.DeviceIdType.MESH,
        )

    def cell_wait(buffer, sem):
        others = buffer.at[pl.ds(0, CELLS - 1)]
        pltpu.make_async_copy(others, others, sem).wait()

    def fwd_start(d, carry):
        cell_copy(fwd_send, fwd_recv, sem_f, d).start()
        return carry

    pl.semaphore_wait(line_sem, 3)
    lax.fori_loop(1, CELLS, fwd_start, 0)
    fwd_recv[me_c] = fwd_send[me_c]

    both = jnp.concatenate([isl_ref[:, 0, :], isl_ref[:, 1, :]], axis=0).astype(F32)
    at_me = jnp.where(iota((LISTS, CELLS), 1) == me_c, both, 0.0)
    tile_half = jnp.sum(at_me, axis=1, keepdims=True)
    tile_col = jnp.concatenate([tile_half, tile_half], axis=0)
    eye = iota((LANES, LANES), 0) == iota((LANES, LANES), 1)
    tile_row = jnp.sum(jnp.where(eye, tile_col, 0.0), axis=0, keepdims=True)
    in_tile = (iota((OWN, LANES), 0).astype(F32) == tile_row).astype(F32)
    order = ord_ref[...].reshape(OWN, CELLS)
    cell_lane = lax.rem(iota((OWN, LANES), 1), CELLS)
    rank = jnp.zeros((OWN, LANES), F32)
    for at in range(CELLS):
        rank = jnp.where(order[:, at : at + 1] == cell_lane, float(at), rank)
    rank_row = jnp.sum(in_tile * rank, axis=0, keepdims=True)
    key_row = 2.0 * rank_row + jnp.where(lane < LISTS, 0.0, 1.0)
    key_col = jnp.sum(jnp.where(eye, key_row, 0.0), axis=1, keepdims=True)
    same = (tile_col == tile_row) & (tile_row >= 0.0)
    ahead = (same & (key_col < key_row)).astype(F32).astype(BF16)
    after = (same & (key_col > key_row)).astype(F32).astype(BF16)
    ahead2 = jnp.concatenate([ahead] * 2, axis=0)
    after2 = jnp.concatenate([after] * 2, axis=0)
    in_tile_b = in_tile.astype(BF16)
    in_tile2 = jnp.concatenate([in_tile_b] * 2, axis=1)
    in_tile2v = jnp.concatenate([in_tile_b] * 2, axis=0)
    tile_int = tile_row.astype(jnp.int32)
    window = lax.rem(me_v, HALF_VIEWS) * ROWS + me_c * OWN + tile_int
    side_at = iota((TSIDE, LANES), 0).astype(F32) + 0.5
    place_x = (lax.rem(window, 32) * TSIDE).astype(F32) + side_at
    place_y = ((window // 32) * TSIDE).astype(F32) + side_at
    acc_ref[...] = jnp.zeros_like(acc_ref)
    sum_ref[...] = jnp.zeros_like(sum_ref)

    cell_wait(fwd_recv, sem_f.at[1])
    v_ref[...] = lists_to_rows(
        jnp.concatenate([fwd_recv[:, 0, :], fwd_recv[:, 1, :]], axis=0)
    )

    def value(kk, j):
        return v_ref[kk * SUB + j : kk * SUB + j + 1, :]

    for kk in range(SUB):
        inv = -0.5 * value(kk, 2)
        dx = place_x - value(kk, 0)
        dy = place_y - value(kk, 1)
        ex_ref[kk] = value(kk, 3) * jnp.exp(inv * (dx * dx))
        ey_ref[kk] = jnp.exp(inv * (dy * dy))
        dy_ref[kk] = dy

    def forward(i, carry):
        rows = pl.ds(pl.multiple_of(i * 64, 64), 64)
        through = jnp.ones((64, LANES), F32)
        second = jnp.ones((64, LANES), F32)
        first = through
        sums = [jnp.zeros((64, LANES), F32) for ch in range(3)]
        for kk in range(SUB):
            ex = ex_ref[kk]
            alpha = jnp.concatenate(
                [ex * ey_ref[kk, pl.ds(4 * i + at, 1), :] for at in range(4)], axis=0
            )
            keep = 1.0 - alpha
            weight = alpha * through
            w_ref[kk, rows, :] = weight
            inverse = pl.reciprocal(keep, approx=True)
            rho_ref[kk, rows, :] = alpha * (inverse * (2.0 - keep * inverse))
            for ch in range(3):
                sums[ch] = sums[ch] + weight * value(kk, 4 + ch)
            through = through * keep
            if kk < 4:
                first = through
            else:
                second = second * keep
        for ch in range(3):
            part_ref[ch, rows, :] = sums[ch]
        pre_ref[rows, :] = jnp.log(first) + jnp.log(second)
        return carry

    lax.fori_loop(0, 4, forward, 0, unroll=True)

    prefix = jnp.exp(dot(jnp.concatenate(split2(pre_ref[...]), axis=1), ahead2))
    pre_ref[...] = prefix
    owed = jnp.zeros((PIX, LANES), F32)
    for ch in range(3):
        seen = prefix * part_ref[ch]
        image = dot(in_tile2, jnp.concatenate(split2(seen), axis=1), ((1,), (1,)))
        rend_ref[pl.ds(2 * ch, OWN, stride=6), :] = image[:, :LANES]
        rend_ref[pl.ds(2 * ch + 1, OWN, stride=6), :] = image[:, LANES:]
        miss = image - tgt_ref[ch].astype(F32)
        miss2 = jnp.concatenate(split2(miss), axis=0)
        pulled = dot(miss2, in_tile2v, ((0,), (0,)))
        gl_ref[ch] = pulled
        owed = owed + seen * pulled
    behind_ref[...] = dot(jnp.concatenate(split2(owed), axis=1), after2)

    def backward(i, carry):
        rows = pl.ds(pl.multiple_of(i * 32, 32), 32)
        prefix = pre_ref[rows, :]
        behind = behind_ref[rows, :]
        pulled = [gl_ref[ch, rows, :] for ch in range(3)]
        for kk in reversed(range(SUB)):
            weight = prefix * w_ref[kk, rows, :]
            tints = [weight * pulled[ch] for ch in range(3)]
            owed = tints[0] * value(kk, 4) + tints[1] * value(kk, 5) + tints[2] * value(kk, 6)
            pull = owed - behind * rho_ref[kk, rows, :]
            behind = behind + owed
            up, down = pull[:16], pull[16:]
            acc_ref[kk] += up + down
            dy_up = dy_ref[kk, pl.ds(2 * i, 1), :]
            dy_down = dy_ref[kk, pl.ds(2 * i + 1, 1), :]
            along_up = (up[:8] + up[8:]) * dy_up
            along_down = (down[:8] + down[8:]) * dy_down
            sum_ref[kk, 0] += along_up + along_down
            sum_ref[kk, 1] += along_up * dy_up + along_down * dy_down
            for ch in range(3):
                tint = tints[ch]
                sum_ref[kk, 2 + ch] += (tint[:8] + tint[8:16]) + (tint[16:24] + tint[24:])
        return carry

    lax.fori_loop(0, 8, backward, 0, unroll=True)

    results = []
    for kk in range(SUB):
        dx = place_x - value(kk, 0)
        inv = value(kk, 2)
        base = acc_ref[kk]
        base_x = base * dx
        base_xx = base_x * dx

        def total(x):
            return jnp.sum(x, axis=0, keepdims=True)

        results += [
            inv * total(base_x),
            inv * total(sum_ref[kk, 0]),
            inv * total((base_xx[:8] + base_xx[8:]) + sum_ref[kk, 1]),
            (1.0 - value(kk, 3)) * total(base),
            total(sum_ref[kk, 2]),
            total(sum_ref[kk, 3]),
            total(sum_ref[kk, 4]),
            jnp.zeros((1, LANES), F32),
        ]
    lists = rows_to_lists(jnp.concatenate(results, axis=0))
    bwd_send[:, 0, :] = lists[:CELLS]
    bwd_send[:, 1, :] = lists[CELLS:]

    def bwd_start(d, carry):
        cell_copy(bwd_send, bwd_recv, sem_b, d).start()
        return carry

    lax.fori_loop(1, CELLS, bwd_start, 0)
    bwd_recv[me_c] = bwd_send[me_c]

    cell_wait(bwd_recv, sem_b.at[1])

    grads = lists_to_rows(jnp.concatenate([bwd_recv[:, 0, :], bwd_recv[:, 1, :]], axis=0))
    last = iota((SUB, LANES), 0) == SUB - 1
    pieces = []
    for kk in range(SUB):
        piece = split2(jnp.where(last, 1.0, grads[kk * SUB : (kk + 1) * SUB]))
        pieces.append([x.astype(F32) for x in piece])
    hot = oh_ref[0:LANES, :]

    def grad_copy(at):
        return pltpu.make_async_remote_copy(
            src_ref=grad_send.at[peers_v[at]],
            dst_ref=grad_recv.at[me_v],
            send_sem=sem_gs.at[at],
            recv_sem=sem_gr.at[me_v],
            device_id=(me_c, peers_v[at]),
            device_id_type=pl.DeviceIdType.MESH,
        )

    def grad_arrived(at):
        return pltpu.make_async_remote_copy(
            src_ref=grad_send.at[peers_v[at]],
            dst_ref=grad_recv.at[peers_v[at]],
            send_sem=sem_gs.at[at],
            recv_sem=sem_gr.at[peers_v[at]],
            device_id=(me_c, peers_v[at]),
            device_id_type=pl.DeviceIdType.MESH,
        )

    for steps, sends in (((2,), (0, 1)), ((1, 3), (2, 3, 4, 5)), ((0,), (6,))):
        homes = [chip_v(step) + core for step in steps for core in range(2)]
        count = len(homes) * SUB
        for kk in range(SUB):
            hi = hi_ref[kk : kk + 1, :]
            for at in range(0, count, 2):
                first = (homes[at // SUB] * SUB + at % SUB).astype(F32)
                here, there = hi == first, hi == first + 1.0
                for part in range(2):
                    lhs_ref[part, at * SUB : (at + 2) * SUB, kk * LANES : (kk + 1) * LANES] = (
                        jnp.concatenate(
                            [
                                jnp.where(here, pieces[kk][part], 0.0),
                                jnp.where(there, pieces[kk][part], 0.0),
                            ],
                            axis=0,
                        ).astype(BF16)
                    )
        rows = slice(0, count * SUB)
        spread = dot(lhs_ref[0, rows, :], hot, ((1,), (1,)))
        spread = spread + dot(lhs_ref[1, rows, :], hot, ((1,), (1,)))
        for which, home in enumerate(homes):
            for at in range(SUB):
                row = (which * SUB + at) * SUB
                grad_send[home, :, at * LANES : (at + 1) * LANES] = spread[row : row + SUB]
        for at in sends:
            grad_copy(at).start()
    grad_recv[me_v] = grad_send[me_v]
    for at in range(VIEWS - 1):
        grad_arrived(at).wait_recv()
    gout_ref[0] = (grad_recv[0] + grad_recv[1]) + (grad_recv[2] + grad_recv[3])
    gout_ref[1] = (grad_recv[4] + grad_recv[5]) + (grad_recv[6] + grad_recv[7])

    for load in loads[7:]:
        load.wait()
    for at in range(VIEWS - 1):
        table_copy(at).wait_send()
        grad_copy(at).wait_send()
    cell_wait(fwd_send, sem_f.at[0])
    cell_wait(bwd_send, sem_b.at[0])


def adam_kernel(
    grad_ref,
    rend_ref,
    basis_ref,
    cam_ref,
    g_ref,
    one_ref,
    two_ref,
    rend_out,
    out_g,
    out_one,
    out_two,
    grads,
    new_g,
    new_one,
    new_two,
    sems,
):
    image = pltpu.make_async_copy(rend_ref, rend_out, sems.at[0, 0])
    image.start()
    touched = grad_ref[0, 7:8, :] + grad_ref[1, 7:8, :] > 0.5
    cameras = [camera_values(cam_ref, which) for which in range(2)]
    fix_one = 1.0 / (1.0 - beta_one**adam_step)
    fix_two = 1.0 / (1.0 - beta_two**adam_step)
    for k in range(3):
        grads[k : k + 1, :] = sum(
            cameras[which][row][k] * grad_ref[which, row : row + 1, :]
            for which in range(2)
            for row in range(2)
        )
    grads[3:5, :] = grad_ref[0, 2:4, :] + grad_ref[1, 2:4, :]
    columns = [basis_ref[which, :, 0:1] for which in range(2)]
    for ch in range(3):
        j = 4 + ch
        grads[5 + 16 * ch : 21 + 16 * ch, :] = (
            columns[0] * grad_ref[0, j : j + 1, :] + columns[1] * grad_ref[1, j : j + 1, :]
        )
    copies = [image]
    for at, (low, high) in enumerate(((0, 16), (16, 32), (32, 48), (48, 53))):
        rows = slice(low, high)
        grad = grads[rows, :]
        first = beta_one * one_ref[rows, :] + (1.0 - beta_one) * grad
        second = beta_two * two_ref[rows, :] + (1.0 - beta_two) * grad * grad
        change = learn_rate * (first * fix_one) / (jnp.sqrt(second * fix_two) + adam_eps)
        new_g[rows, :] = jnp.where(touched, g_ref[rows, :] - change, g_ref[rows, :])
        new_one[rows, :] = jnp.where(touched, first, one_ref[rows, :])
        new_two[rows, :] = jnp.where(touched, second, two_ref[rows, :])
        for which, (source, target) in enumerate(
            ((new_g, out_g), (new_one, out_one), (new_two, out_two))
        ):
            copy = pltpu.make_async_copy(
                source.at[pl.ds(low, high - low), :],
                target.at[pl.ds(low, high - low), :],
                sems.at[1 + at, which],
            )
            copy.start()
            copies.append(copy)
    for copy in copies:
        copy.wait()


def per_device(
    gaussians,
    moment_one,
    moment_two,
    cameras,
    target,
    gauss_ids,
    tile_counts,
    intersection_slots,
    depth_order,
):
    vmem = pl.BlockSpec(memory_space=pltpu.VMEM)
    hbm = pl.BlockSpec(memory_space=pltpu.HBM)
    shape = jax.ShapeDtypeStruct(gaussians.shape, F32)
    sems = pltpu.SemaphoreType.DMA
    rendered, grads, basis, cameras, gaussians, moment_one, moment_two = pl.pallas_call(
        step_kernel,
        out_shape=(
            jax.ShapeDtypeStruct((96, LANES), F32),
            jax.ShapeDtypeStruct((2, SUB, HOME), F32),
            jax.ShapeDtypeStruct((2, 16, LANES), F32),
            jax.ShapeDtypeStruct((2, 2, 4), F32),
            shape,
            shape,
            shape,
        ),
        in_specs=[hbm] * 9,
        out_specs=(vmem,) * 7,
        scratch_shapes=[
            pltpu.VMEM((3, OWN, PIX), BF16),
            pltpu.VMEM((16, ROWS), jnp.int32),
            pltpu.VMEM((1, ROWS), jnp.int32),
            pltpu.VMEM((CELLS, 2, CELLS), jnp.int32),
            pltpu.VMEM((OWN, 1, CELLS), jnp.int32),
            pltpu.VMEM((2, SUB, HOME), F32),
            pltpu.VMEM((VIEWS, SUB, HOME), F32),
            pltpu.VMEM((CELLS, 2, LANES), F32),
            pltpu.VMEM((CELLS, 2, LANES), F32),
            pltpu.VMEM((CELLS, 2, LANES), F32),
            pltpu.VMEM((CELLS, 2, LANES), F32),
            pltpu.VMEM((VIEWS, SUB, HOME), F32),
            pltpu.VMEM((VIEWS, SUB, HOME), F32),
            pltpu.VMEM((3 * LANES, SUB * LANES), BF16),
            pltpu.VMEM((SUB, LANES), F32),
            pltpu.VMEM((64, LANES), F32),
            pltpu.VMEM((SUB, TSIDE, LANES), F32),
            pltpu.VMEM((SUB, TSIDE, LANES), F32),
            pltpu.VMEM((SUB, TSIDE, LANES), F32),
            pltpu.VMEM((SUB, PIX, LANES), F32),
            pltpu.VMEM((SUB, PIX, LANES), F32),
            pltpu.VMEM((3, PIX, LANES), F32),
            pltpu.VMEM((PIX, LANES), F32),
            pltpu.VMEM((PIX, LANES), F32),
            pltpu.VMEM((3, PIX, LANES), F32),
            pltpu.VMEM((SUB, TSIDE, LANES), F32),
            pltpu.VMEM((SUB, 5, SUB, LANES), F32),
            pltpu.VMEM((2, HIGHS * SUB // 2, SUB * LANES), BF16),
            sems((VIEWS,)),
            sems((VIEWS,)),
            sems((2,)),
            sems((2,)),
            sems((VIEWS,)),
            sems((VIEWS,)),
            sems((9,)),
            pltpu.SemaphoreType.REGULAR,
            pltpu.SemaphoreType.REGULAR,
        ],
        compiler_params=pltpu.CompilerParams(
            collective_id=0, has_side_effects=True, vmem_limit_bytes=40 * 1024 * 1024
        ),
        name="splat_step",
    )(
        *(
            pltpu.with_memory_space_constraint(x, pltpu.HBM)
            for x in (
                gaussians,
                moment_one,
                moment_two,
                cameras,
                jnp.transpose(target[:, 0], (1, 0, 2)),
                jnp.transpose(gauss_ids[0, :, 0, :], (1, 0)),
                tile_counts.reshape(1, ROWS),
                jnp.transpose(intersection_slots[:, :, 0, :], (0, 2, 1)),
                depth_order,
            )
        )
    )
    image, new_gaussians, new_one, new_two = pl.pallas_call(
        adam_kernel,
        out_shape=(jax.ShapeDtypeStruct((96, LANES), F32), shape, shape, shape),
        in_specs=[vmem] * 7,
        out_specs=(hbm,) * 4,
        scratch_shapes=[
            pltpu.VMEM((56, HOME), F32),
            pltpu.VMEM(gaussians.shape, F32),
            pltpu.VMEM(gaussians.shape, F32),
            pltpu.VMEM(gaussians.shape, F32),
            sems((5, 3)),
        ],
        compiler_params=pltpu.CompilerParams(vmem_limit_bytes=20 * 1024 * 1024),
        name="adam",
    )(grads, rendered, basis, cameras, gaussians, moment_one, moment_two)
    return (image.reshape(OWN, 1, 3, PIX), new_gaussians, new_one, new_two)


def solution(mesh):
    placed = (
        P(None, ("cell", "view")),
        P(None, ("cell", "view")),
        P(None, ("cell", "view")),
        P(),
        P("cell", "view", None, None),
        P("cell", None, "view", None),
        P("cell", None, "view"),
        P(None, None, "view", None),
        P("cell", "view", None),
    )
    return jax.shard_map(
        per_device,
        mesh=mesh,
        in_specs=placed,
        out_specs=(
            P("cell", "view", None, None),
            P(None, ("cell", "view")),
            P(None, ("cell", "view")),
            P(None, ("cell", "view")),
        ),
        check_vma=False,
    )
```

```python
import jax
import jax.numpy as jnp
from jax import lax
from jax.experimental import pallas as pl
from jax.experimental.pallas import tpu as pltpu
from jax.sharding import PartitionSpec as P

CELLS = 32
VIEWS = 8
HALF_VIEWS = VIEWS // 2
HOME = 1024
OWN = 16
ROWS = 512
PIX = 256
TSIDE = 16
LISTS = 2 * CELLS
SUB = 8
LANES = 128
HIGHS = VIEWS * SUB
F32 = jnp.float32
BF16 = jnp.bfloat16
LARGE = 1e38

band_zero = 0.28209479177387814
band_one = 0.4886025119029199
band_two = (
    1.0925484305920792,
    -1.0925484305920792,
    0.31539156525252005,
    -1.0925484305920792,
    0.5462742152960396,
)
band_three = (
    -0.5900435899266435,
    2.890611442640554,
    -0.4570457994644658,
    0.3731763325901154,
    -0.4570457994644658,
    1.445305721320277,
    -0.5900435899266435,
)
beta_one = 0.9
beta_two = 0.999
learn_rate = 0.01
adam_eps = 1e-08
adam_step = 10.0


def iota(shape, axis):
    return lax.broadcasted_iota(jnp.int32, shape, axis)


def camera_values(cam_ref, which):
    return [[cam_ref[which, row : row + 1, k : k + 1] for k in range(4)] for row in range(2)]


def basis_column(camera):
    a, b = camera
    nx = a[1] * b[2] - a[2] * b[1]
    ny = a[2] * b[0] - a[0] * b[2]
    nz = a[0] * b[1] - a[1] * b[0]
    norm = jnp.sqrt(nx * nx + ny * ny + nz * nz)
    x, y, z = nx / norm, ny / norm, nz / norm
    xx, yy, zz = x * x, y * y, z * z
    terms = [
        x * 0.0 + band_zero,
        -band_one * y,
        band_one * z,
        -band_one * x,
        band_two[0] * x * y,
        band_two[1] * y * z,
        band_two[2] * (2.0 * zz - xx - yy),
        band_two[3] * x * z,
        band_two[4] * (xx - yy),
        band_three[0] * y * (3.0 * xx - yy),
        band_three[1] * x * y * z,
        band_three[2] * y * (4.0 * zz - xx - yy),
        band_three[3] * z * (2.0 * zz - 3.0 * xx - 3.0 * yy),
        band_three[4] * x * (4.0 * zz - xx - yy),
        band_three[5] * z * (xx - yy),
        band_three[6] * x * (xx - 3.0 * yy),
    ]
    row = iota((16, 1), 0)
    column = jnp.zeros((16, 1), F32)
    for at, term in enumerate(terms):
        column = jnp.where(row == at, term, column)
    return column


def split3(x):
    high = x.astype(BF16)
    rest = x - high.astype(F32)
    mid = rest.astype(BF16)
    low = (rest - mid.astype(F32)).astype(BF16)
    return high, mid, low


def split2(x):
    high = x.astype(BF16)
    return high, (x - high.astype(F32)).astype(BF16)


def dot(a, b, dims=((1,), (0,))):
    return lax.dot_general(a, b, (dims, ((), ())), preferred_element_type=F32)


def rows_to_lists(x):
    t = x.T
    return jnp.concatenate([t[:LISTS], t[LISTS:]], axis=1)


def lists_to_rows(x):
    t = x.T
    return jnp.concatenate([t[:64], t[64:]], axis=1)


def step_kernel(
    g_hbm,
    one_hbm,
    two_hbm,
    cam_hbm,
    tgt_hbm,
    ids_hbm,
    cnt_hbm,
    isl_hbm,
    ord_hbm,
    rend_ref,
    gout_ref,
    basis_ref,
    cam_ref,
    g_ref,
    one_ref,
    two_ref,
    tgt_ref,
    ids_ref,
    cnt_ref,
    isl_ref,
    ord_ref,
    tab_send,
    tab_recv,
    fwd_send,
    fwd_recv,
    bwd_send,
    bwd_recv,
    grad_send,
    grad_recv,
    oh_ref,
    oht_ref,
    hi_ref,
    v_ref,
    ex_ref,
    ey_ref,
    dy_ref,
    w_ref,
    rho_ref,
    part_ref,
    pre_ref,
    behind_ref,
    gl_ref,
    acc_ref,
    sum_ref,
    lhs_ref,
    sem_ts,
    sem_tr,
    sem_f,
    sem_b,
    sem_gs,
    sem_gr,
    sem_in,
    near_sem,
    line_sem,
):
    loads = [
        pltpu.make_async_copy(source, target, sem_in.at[at])
        for at, (source, target) in enumerate(
            (
                (g_hbm, g_ref),
                (cam_hbm, cam_ref),
                (isl_hbm, isl_ref),
                (ids_hbm, ids_ref),
                (cnt_hbm, cnt_ref),
                (ord_hbm, ord_ref),
                (tgt_hbm, tgt_ref),
                (one_hbm, one_ref),
                (two_hbm, two_ref),
            )
        )
    ]
    for load in loads[:7]:
        load.start()
    me_c = lax.axis_index("cell")
    me_v = lax.axis_index("view")

    def peer_c(d):
        return lax.rem(me_c + lax.rem(d + 10, CELLS - 1) + 1, CELLS)

    me_x, me_core = me_v // 2, lax.rem(me_v, 2)
    me_y, me_z = me_c // 8, lax.rem(me_c, 8)

    def chip_v(step):
        return 2 * lax.rem(me_x + step, 4)

    peers_v = [chip_v(step) + core for step in (2, 1, 3) for core in range(2)]
    peers_v.append(me_v + 1 - 2 * me_core)

    def near_z(d):
        return me_y * 8 + lax.rem(me_z + d + 1 + 3 * (d // 2), 8)

    def line_y(d):
        return lax.rem(me_y + d, 4) * 8 + me_z

    def signal(sem, cell):
        pl.semaphore_signal(
            sem, inc=1, device_id=(cell, me_v), device_id_type=pl.DeviceIdType.MESH
        )

    barrier = pltpu.get_barrier_semaphore()

    def greet_z(sem):
        def body(d, carry):
            signal(sem, near_z(d))
            return carry

        lax.fori_loop(0, 4, body, 0)

    def greet_y(sem):
        def body(d, carry):
            signal(sem, line_y(d))
            return carry

        lax.fori_loop(1, 4, body, 0)

    greet_z(barrier)
    greet_y(barrier)
    for peer in peers_v:
        pl.semaphore_signal(
            barrier, inc=1, device_id=(me_c, peer), device_id_type=pl.DeviceIdType.MESH
        )
    for load in loads[:7]:
        load.wait()
    for load in loads[7:]:
        load.start()

    centre = [g_ref[k : k + 1, :] for k in range(3)]
    inv_var = jnp.exp(-2.0 * g_ref[3:4, :])
    opacity = 1.0 / (1.0 + jnp.exp(-g_ref[4:5, :]))
    for which in range(2):
        camera = camera_values(cam_ref, which)
        column = basis_column(camera)
        basis_ref[which] = jnp.broadcast_to(column, (16, LANES))
        screen = [
            row[0] * centre[0] + row[1] * centre[1] + row[2] * centre[2] + row[3] for row in camera
        ]
        colour = [
            0.5 + jnp.sum(g_ref[5 + 16 * ch : 21 + 16 * ch, :] * column, axis=0, keepdims=True)
            for ch in range(3)
        ]
        table = jnp.concatenate(
            screen + [inv_var, opacity] + colour + [jnp.zeros((1, HOME), F32)], axis=0
        )
        table = jnp.clip(table, -LARGE, LARGE)
        tab_send[which] = jnp.where(table == table, table, 0.0)

    lane = iota((1, LANES), 1)
    mine = isl_ref[me_c]
    offsets = jnp.concatenate([mine[0:1], mine[1:2], mine[0:1], mine[1:2]], axis=1)
    wanted = jnp.where(offsets >= 0, lax.rem(lane, CELLS) * OWN + offsets, -1)
    pick = (iota((ROWS, LANES), 0) == wanted).astype(F32).astype(BF16)
    all_ids = ids_ref[...]
    packed = jnp.concatenate(
        [
            (all_ids // LANES).astype(F32),
            lax.rem(all_ids, LANES).astype(F32),
            jnp.broadcast_to(cnt_ref[...].astype(F32), (16, ROWS)),
        ],
        axis=0,
    ).astype(BF16)
    picked = dot(packed, pick)
    left = iota((SUB, LANES), 1) < LISTS
    high = jnp.where(left, picked[0:8], picked[8:16])
    low = jnp.where(left, picked[16:24], picked[24:32])
    slot = iota((SUB, LANES), 0) + jnp.where(left, 0, SUB)
    live = slot.astype(F32) < picked[32:40]
    high = jnp.where(live, high, -1.0)
    hi_ref[...] = high
    for kk in range(SUB):
        hot = (iota((LANES, LANES), 0).astype(F32) == low[kk : kk + 1]).astype(F32)
        oht_ref[kk * LANES : (kk + 1) * LANES, :] = hot.T.astype(BF16)
        hot = hot.astype(BF16)
        for part in range(3):
            oh_ref[part * LANES : (part + 1) * LANES, kk * LANES : (kk + 1) * LANES] = hot

    pl.semaphore_wait(barrier, VIEWS - 1 + 7)
    signal(near_sem, near_z(1))
    signal(near_sem, near_z(2))

    def table_copy(at):
        to = peers_v[at]
        return pltpu.make_async_remote_copy(
            src_ref=tab_send.at[to // HALF_VIEWS],
            dst_ref=tab_recv.at[me_v],
            send_sem=sem_ts.at[at],
            recv_sem=sem_tr.at[me_v],
            device_id=(me_c, to),
            device_id_type=pl.DeviceIdType.MESH,
        )

    def table_wait(at):
        pltpu.make_async_remote_copy(
            src_ref=tab_send.at[0],
            dst_ref=tab_recv.at[peers_v[at]],
            send_sem=sem_ts.at[at],
            recv_sem=sem_tr.at[peers_v[at]],
            device_id=(me_c, peers_v[at]),
            device_id_type=pl.DeviceIdType.MESH,
        ).wait_recv()

    for at in range(VIEWS - 1):
        table_copy(at).start()
    tab_recv[me_v] = tab_send[me_v // HALF_VIEWS]

    chosen = [jnp.zeros((SUB, LANES), F32) for kk in range(SUB)]
    for group, (steps, arrivals) in enumerate((((0,), (6,)), ((1, 3), (2, 3, 4, 5)), ((2,), (0, 1)))):
        for at in arrivals:
            table_wait(at)
        if group == 0:
            pl.semaphore_wait(near_sem, 2)
            greet_y(line_sem)
        blocks, highs = [], []
        for step in steps:
            for core in range(2):
                home = chip_v(step) + core
                for at in range(SUB):
                    blocks.append(tab_recv[home, :, at * LANES : (at + 1) * LANES])
                    highs.append((home * SUB + at).astype(F32))
        lhs = jnp.concatenate(split3(jnp.concatenate(blocks, axis=0)), axis=1)
        for pair in range(4):
            got = dot(lhs, oh_ref[:, pair * 256 : (pair + 1) * 256])
            for side in range(2):
                kk = 2 * pair + side
                hi = hi_ref[kk : kk + 1, :]
                for at, value_at in enumerate(highs):
                    chosen[kk] = chosen[kk] + jnp.where(
                        hi == value_at,
                        got[at * SUB : (at + 1) * SUB, side * LANES : (side + 1) * LANES],
                        0.0,
                    )
    lists = rows_to_lists(jnp.concatenate(chosen, axis=0))
    fwd_send[:, 0, :] = lists[:CELLS]
    fwd_send[:, 1, :] = lists[CELLS:]

    def cell_copy(source, target, sems, d):
        return pltpu.make_async_remote_copy(
            src_ref=source.at[peer_c(d)],
            dst_ref=target.at[me_c],
            send_sem=sems.at[0],
            recv_sem=sems.at[1],
            device_id=(peer_c(d), me_v),
            device_id_type=pl.DeviceIdType.MESH,
        )

    def cell_wait(buffer, sem):
        others = buffer.at[pl.ds(0, CELLS - 1)]
        pltpu.make_async_copy(others, others, sem).wait()

    def fwd_start(d, carry):
        cell_copy(fwd_send, fwd_recv, sem_f, d).start()
        return carry

    pl.semaphore_wait(line_sem, 3)
    lax.fori_loop(1, CELLS, fwd_start, 0)
    fwd_recv[me_c] = fwd_send[me_c]

    both = jnp.concatenate([isl_ref[:, 0, :], isl_ref[:, 1, :]], axis=0).astype(F32)
    at_me = jnp.where(iota((LISTS, CELLS), 1) == me_c, both, 0.0)
    tile_half = jnp.sum(at_me, axis=1, keepdims=True)
    tile_col = jnp.concatenate([tile_half, tile_half], axis=0)
    eye = iota((LANES, LANES), 0) == iota((LANES, LANES), 1)
    tile_row = jnp.sum(jnp.where(eye, tile_col, 0.0), axis=0, keepdims=True)
    in_tile = (iota((OWN, LANES), 0).astype(F32) == tile_row).astype(F32)
    order = ord_ref[...].reshape(OWN, CELLS)
    cell_lane = lax.rem(iota((OWN, LANES), 1), CELLS)
    rank = jnp.zeros((OWN, LANES), F32)
    for at in range(CELLS):
        rank = jnp.where(order[:, at : at + 1] == cell_lane, float(at), rank)
    rank_row = jnp.sum(in_tile * rank, axis=0, keepdims=True)
    key_row = 2.0 * rank_row + jnp.where(lane < LISTS, 0.0, 1.0)
    key_col = jnp.sum(jnp.where(eye, key_row, 0.0), axis=1, keepdims=True)
    same = (tile_col == tile_row) & (tile_row >= 0.0)
    ahead = (same & (key_col < key_row)).astype(F32).astype(BF16)
    after = (same & (key_col > key_row)).astype(F32).astype(BF16)
    ahead2 = jnp.concatenate([ahead] * 2, axis=0)
    after2 = jnp.concatenate([after] * 2, axis=0)
    in_tile_b = in_tile.astype(BF16)
    in_tile2 = jnp.concatenate([in_tile_b] * 2, axis=1)
    in_tile2v = jnp.concatenate([in_tile_b] * 2, axis=0)
    tile_int = tile_row.astype(jnp.int32)
    window = lax.rem(me_v, HALF_VIEWS) * ROWS + me_c * OWN + tile_int
    side_at = iota((TSIDE, LANES), 0).astype(F32) + 0.5
    place_x = (lax.rem(window, 32) * TSIDE).astype(F32) + side_at
    place_y = ((window // 32) * TSIDE).astype(F32) + side_at
    acc_ref[...] = jnp.zeros_like(acc_ref)
    sum_ref[...] = jnp.zeros_like(sum_ref)

    cell_wait(fwd_recv, sem_f.at[1])
    v_ref[...] = lists_to_rows(
        jnp.concatenate([fwd_recv[:, 0, :], fwd_recv[:, 1, :]], axis=0)
    )

    def value(kk, j):
        return v_ref[kk * SUB + j : kk * SUB + j + 1, :]

    for kk in range(SUB):
        inv = -0.5 * value(kk, 2)
        dx = place_x - value(kk, 0)
        dy = place_y - value(kk, 1)
        ex_ref[kk] = value(kk, 3) * jnp.exp(inv * (dx * dx))
        ey_ref[kk] = jnp.exp(inv * (dy * dy))
        dy_ref[kk] = dy

    def forward(i, carry):
        rows = pl.ds(pl.multiple_of(i * 64, 64), 64)
        through = jnp.ones((64, LANES), F32)
        second = jnp.ones((64, LANES), F32)
        first = through
        sums = [jnp.zeros((64, LANES), F32) for ch in range(3)]
        for kk in range(SUB):
            ex = ex_ref[kk]
            alpha = jnp.concatenate(
                [ex * ey_ref[kk, pl.ds(4 * i + at, 1), :] for at in range(4)], axis=0
            )
            keep = 1.0 - alpha
            weight = alpha * through
            w_ref[kk, rows, :] = weight
            inverse = pl.reciprocal(keep, approx=True)
            rho_ref[kk, rows, :] = alpha * (inverse * (2.0 - keep * inverse))
            for ch in range(3):
                sums[ch] = sums[ch] + weight * value(kk, 4 + ch)
            through = through * keep
            if kk < 4:
                first = through
            else:
                second = second * keep
        for ch in range(3):
            part_ref[ch, rows, :] = sums[ch]
        pre_ref[rows, :] = jnp.log(first) + jnp.log(second)
        return carry

    lax.fori_loop(0, 4, forward, 0, unroll=True)

    prefix = jnp.exp(dot(jnp.concatenate(split2(pre_ref[...]), axis=1), ahead2))
    pre_ref[...] = prefix
    owed = jnp.zeros((PIX, LANES), F32)
    for ch in range(3):
        seen = prefix * part_ref[ch]
        image = dot(in_tile2, jnp.concatenate(split2(seen), axis=1), ((1,), (1,)))
        rend_ref[pl.ds(2 * ch, OWN, stride=6), :] = image[:, :LANES]
        rend_ref[pl.ds(2 * ch + 1, OWN, stride=6), :] = image[:, LANES:]
        miss = image - tgt_ref[ch].astype(F32)
        miss2 = jnp.concatenate(split2(miss), axis=0)
        pulled = dot(miss2, in_tile2v, ((0,), (0,)))
        gl_ref[ch] = pulled
        owed = owed + seen * pulled
    behind_ref[...] = dot(jnp.concatenate(split2(owed), axis=1), after2)

    def backward(i, carry):
        rows = pl.ds(pl.multiple_of(i * 32, 32), 32)
        prefix = pre_ref[rows, :]
        behind = behind_ref[rows, :]
        pulled = [gl_ref[ch, rows, :] for ch in range(3)]
        for kk in reversed(range(SUB)):
            weight = prefix * w_ref[kk, rows, :]
            tints = [weight * pulled[ch] for ch in range(3)]
            owed = tints[0] * value(kk, 4) + tints[1] * value(kk, 5) + tints[2] * value(kk, 6)
            pull = owed - behind * rho_ref[kk, rows, :]
            behind = behind + owed
            up, down = pull[:16], pull[16:]
            acc_ref[kk] += up + down
            dy_up = dy_ref[kk, pl.ds(2 * i, 1), :]
            dy_down = dy_ref[kk, pl.ds(2 * i + 1, 1), :]
            along_up = (up[:8] + up[8:]) * dy_up
            along_down = (down[:8] + down[8:]) * dy_down
            sum_ref[kk, 0] += along_up + along_down
            sum_ref[kk, 1] += along_up * dy_up + along_down * dy_down
            for ch in range(3):
                tint = tints[ch]
                sum_ref[kk, 2 + ch] += (tint[:8] + tint[8:16]) + (tint[16:24] + tint[24:])
        return carry

    lax.fori_loop(0, 8, backward, 0, unroll=True)

    results = []
    for kk in range(SUB):
        dx = place_x - value(kk, 0)
        inv = value(kk, 2)
        base = acc_ref[kk]
        base_x = base * dx
        base_xx = base_x * dx

        def total(x):
            return jnp.sum(x, axis=0, keepdims=True)

        results += [
            inv * total(base_x),
            inv * total(sum_ref[kk, 0]),
            inv * total((base_xx[:8] + base_xx[8:]) + sum_ref[kk, 1]),
            (1.0 - value(kk, 3)) * total(base),
            total(sum_ref[kk, 2]),
            total(sum_ref[kk, 3]),
            total(sum_ref[kk, 4]),
            jnp.zeros((1, LANES), F32),
        ]
    lists = rows_to_lists(jnp.concatenate(results, axis=0))
    bwd_send[:, 0, :] = lists[:CELLS]
    bwd_send[:, 1, :] = lists[CELLS:]

    def bwd_start(d, carry):
        cell_copy(bwd_send, bwd_recv, sem_b, d).start()
        return carry

    lax.fori_loop(1, CELLS, bwd_start, 0)
    bwd_recv[me_c] = bwd_send[me_c]

    cell_wait(bwd_recv, sem_b.at[1])

    grads = lists_to_rows(jnp.concatenate([bwd_recv[:, 0, :], bwd_recv[:, 1, :]], axis=0))
    last = iota((SUB, LANES), 0) == SUB - 1
    pieces = []
    for kk in range(SUB):
        piece = split2(jnp.where(last, 1.0, grads[kk * SUB : (kk + 1) * SUB]))
        pieces.append([x.astype(F32) for x in piece])
    hot = oht_ref[...]

    def grad_copy(at):
        return pltpu.make_async_remote_copy(
            src_ref=grad_send.at[peers_v[at]],
            dst_ref=grad_recv.at[me_v],
            send_sem=sem_gs.at[at],
            recv_sem=sem_gr.at[me_v],
            device_id=(me_c, peers_v[at]),
            device_id_type=pl.DeviceIdType.MESH,
        )

    def grad_arrived(at):
        return pltpu.make_async_remote_copy(
            src_ref=grad_send.at[peers_v[at]],
            dst_ref=grad_recv.at[peers_v[at]],
            send_sem=sem_gs.at[at],
            recv_sem=sem_gr.at[peers_v[at]],
            device_id=(me_c, peers_v[at]),
            device_id_type=pl.DeviceIdType.MESH,
        )

    for steps, sends in (((2,), (0, 1)), ((1, 3), (2, 3, 4, 5)), ((0,), (6,))):
        homes = [chip_v(step) + core for step in steps for core in range(2)]
        count = len(homes) * SUB
        for kk in range(SUB):
            hi = hi_ref[kk : kk + 1, :]
            for at in range(0, count, 2):
                first = (homes[at // SUB] * SUB + at % SUB).astype(F32)
                here, there = hi == first, hi == first + 1.0
                for part in range(2):
                    lhs_ref[part, at * SUB : (at + 2) * SUB, kk * LANES : (kk + 1) * LANES] = (
                        jnp.concatenate(
                            [
                                jnp.where(here, pieces[kk][part], 0.0),
                                jnp.where(there, pieces[kk][part], 0.0),
                            ],
                            axis=0,
                        ).astype(BF16)
                    )
        rows = slice(0, count * SUB)
        spread = dot(lhs_ref[0, rows, :], hot)
        spread = spread + dot(lhs_ref[1, rows, :], hot)
        for which, home in enumerate(homes):
            for at in range(SUB):
                row = (which * SUB + at) * SUB
                grad_send[home, :, at * LANES : (at + 1) * LANES] = spread[row : row + SUB]
        for at in sends:
            grad_copy(at).start()
    grad_recv[me_v] = grad_send[me_v]
    for at in range(VIEWS - 1):
        grad_arrived(at).wait_recv()
    gout_ref[0] = (grad_recv[0] + grad_recv[1]) + (grad_recv[2] + grad_recv[3])
    gout_ref[1] = (grad_recv[4] + grad_recv[5]) + (grad_recv[6] + grad_recv[7])

    for load in loads[7:]:
        load.wait()
    for at in range(VIEWS - 1):
        table_copy(at).wait_send()
        grad_copy(at).wait_send()
    cell_wait(fwd_send, sem_f.at[0])
    cell_wait(bwd_send, sem_b.at[0])


def adam_kernel(
    grad_ref,
    rend_ref,
    basis_ref,
    cam_ref,
    g_ref,
    one_ref,
    two_ref,
    rend_out,
    out_g,
    out_one,
    out_two,
    grads,
    new_g,
    new_one,
    new_two,
    sems,
):
    image = pltpu.make_async_copy(rend_ref, rend_out, sems.at[0, 0])
    image.start()
    touched = grad_ref[0, 7:8, :] + grad_ref[1, 7:8, :] > 0.5
    cameras = [camera_values(cam_ref, which) for which in range(2)]
    fix_one = 1.0 / (1.0 - beta_one**adam_step)
    fix_two = 1.0 / (1.0 - beta_two**adam_step)
    for k in range(3):
        grads[k : k + 1, :] = sum(
            cameras[which][row][k] * grad_ref[which, row : row + 1, :]
            for which in range(2)
            for row in range(2)
        )
    grads[3:5, :] = grad_ref[0, 2:4, :] + grad_ref[1, 2:4, :]
    columns = [basis_ref[which, :, 0:1] for which in range(2)]
    for ch in range(3):
        j = 4 + ch
        grads[5 + 16 * ch : 21 + 16 * ch, :] = (
            columns[0] * grad_ref[0, j : j + 1, :] + columns[1] * grad_ref[1, j : j + 1, :]
        )
    copies = [image]
    for at, (low, high) in enumerate(((0, 16), (16, 32), (32, 48), (48, 53))):
        rows = slice(low, high)
        grad = grads[rows, :]
        first = beta_one * one_ref[rows, :] + (1.0 - beta_one) * grad
        second = beta_two * two_ref[rows, :] + (1.0 - beta_two) * grad * grad
        change = learn_rate * (first * fix_one) / (jnp.sqrt(second * fix_two) + adam_eps)
        new_g[rows, :] = jnp.where(touched, g_ref[rows, :] - change, g_ref[rows, :])
        new_one[rows, :] = jnp.where(touched, first, one_ref[rows, :])
        new_two[rows, :] = jnp.where(touched, second, two_ref[rows, :])
        for which, (source, target) in enumerate(
            ((new_g, out_g), (new_one, out_one), (new_two, out_two))
        ):
            copy = pltpu.make_async_copy(
                source.at[pl.ds(low, high - low), :],
                target.at[pl.ds(low, high - low), :],
                sems.at[1 + at, which],
            )
            copy.start()
            copies.append(copy)
    for copy in copies:
        copy.wait()


def per_device(
    gaussians,
    moment_one,
    moment_two,
    cameras,
    target,
    gauss_ids,
    tile_counts,
    intersection_slots,
    depth_order,
):
    vmem = pl.BlockSpec(memory_space=pltpu.VMEM)
    hbm = pl.BlockSpec(memory_space=pltpu.HBM)
    shape = jax.ShapeDtypeStruct(gaussians.shape, F32)
    sems = pltpu.SemaphoreType.DMA
    rendered, grads, basis, cameras, gaussians, moment_one, moment_two = pl.pallas_call(
        step_kernel,
        out_shape=(
            jax.ShapeDtypeStruct((96, LANES), F32),
            jax.ShapeDtypeStruct((2, SUB, HOME), F32),
            jax.ShapeDtypeStruct((2, 16, LANES), F32),
            jax.ShapeDtypeStruct((2, 2, 4), F32),
            shape,
            shape,
            shape,
        ),
        in_specs=[hbm] * 9,
        out_specs=(vmem,) * 7,
        scratch_shapes=[
            pltpu.VMEM((3, OWN, PIX), BF16),
            pltpu.VMEM((16, ROWS), jnp.int32),
            pltpu.VMEM((1, ROWS), jnp.int32),
            pltpu.VMEM((CELLS, 2, CELLS), jnp.int32),
            pltpu.VMEM((OWN, 1, CELLS), jnp.int32),
            pltpu.VMEM((2, SUB, HOME), F32),
            pltpu.VMEM((VIEWS, SUB, HOME), F32),
            pltpu.VMEM((CELLS, 2, LANES), F32),
            pltpu.VMEM((CELLS, 2, LANES), F32),
            pltpu.VMEM((CELLS, 2, LANES), F32),
            pltpu.VMEM((CELLS, 2, LANES), F32),
            pltpu.VMEM((VIEWS, SUB, HOME), F32),
            pltpu.VMEM((VIEWS, SUB, HOME), F32),
            pltpu.VMEM((3 * LANES, SUB * LANES), BF16),
            pltpu.VMEM((SUB * LANES, LANES), BF16),
            pltpu.VMEM((SUB, LANES), F32),
            pltpu.VMEM((64, LANES), F32),
            pltpu.VMEM((SUB, TSIDE, LANES), F32),
            pltpu.VMEM((SUB, TSIDE, LANES), F32),
            pltpu.VMEM((SUB, TSIDE, LANES), F32),
            pltpu.VMEM((SUB, PIX, LANES), F32),
            pltpu.VMEM((SUB, PIX, LANES), F32),
            pltpu.VMEM((3, PIX, LANES), F32),
            pltpu.VMEM((PIX, LANES), F32),
            pltpu.VMEM((PIX, LANES), F32),
            pltpu.VMEM((3, PIX, LANES), F32),
            pltpu.VMEM((SUB, TSIDE, LANES), F32),
            pltpu.VMEM((SUB, 5, SUB, LANES), F32),
            pltpu.VMEM((2, HIGHS * SUB // 2, SUB * LANES), BF16),
            sems((VIEWS,)),
            sems((VIEWS,)),
            sems((2,)),
            sems((2,)),
            sems((VIEWS,)),
            sems((VIEWS,)),
            sems((9,)),
            pltpu.SemaphoreType.REGULAR,
            pltpu.SemaphoreType.REGULAR,
        ],
        compiler_params=pltpu.CompilerParams(
            collective_id=0, has_side_effects=True, vmem_limit_bytes=40 * 1024 * 1024
        ),
        name="splat_step",
    )(
        *(
            pltpu.with_memory_space_constraint(x, pltpu.HBM)
            for x in (
                gaussians,
                moment_one,
                moment_two,
                cameras,
                jnp.transpose(target[:, 0], (1, 0, 2)),
                jnp.transpose(gauss_ids[0, :, 0, :], (1, 0)),
                tile_counts.reshape(1, ROWS),
                jnp.transpose(intersection_slots[:, :, 0, :], (0, 2, 1)),
                depth_order,
            )
        )
    )
    image, new_gaussians, new_one, new_two = pl.pallas_call(
        adam_kernel,
        out_shape=(jax.ShapeDtypeStruct((96, LANES), F32), shape, shape, shape),
        in_specs=[vmem] * 7,
        out_specs=(hbm,) * 4,
        scratch_shapes=[
            pltpu.VMEM((56, HOME), F32),
            pltpu.VMEM(gaussians.shape, F32),
            pltpu.VMEM(gaussians.shape, F32),
            pltpu.VMEM(gaussians.shape, F32),
            sems((5, 3)),
        ],
        compiler_params=pltpu.CompilerParams(vmem_limit_bytes=20 * 1024 * 1024),
        name="adam",
    )(grads, rendered, basis, cameras, gaussians, moment_one, moment_two)
    return (image.reshape(OWN, 1, 3, PIX), new_gaussians, new_one, new_two)


def solution(mesh):
    placed = (
        P(None, ("cell", "view")),
        P(None, ("cell", "view")),
        P(None, ("cell", "view")),
        P(),
        P("cell", "view", None, None),
        P("cell", None, "view", None),
        P("cell", None, "view"),
        P(None, None, "view", None),
        P("cell", "view", None),
    )
    return jax.shard_map(
        per_device,
        mesh=mesh,
        in_specs=placed,
        out_specs=(
            P("cell", "view", None, None),
            P(None, ("cell", "view")),
            P(None, ("cell", "view")),
            P(None, ("cell", "view")),
        ),
        check_vma=False,
    )
```
